256 devices in a mesh: layer: 8 (over z), tok: 32 (over x, y, core).
Axes of the slice: x: 4, y: 4, z: 8, core: 2. Of those that a mesh axis runs over, the one named last changes fastest.
Arguments:
- acts: bfloat16 [8, 1024, 4096], P('layer', 'tok'), may hold values from -6 to 6
- targets: bfloat16 [8, 1024, 4096], P('layer', 'tok'), may hold values from -6 to 6
- enc_weight: bfloat16 [8, 2048, 4096], P('layer', 'tok'), may hold values from -0.09375 to 0.09375
- enc_bias: float32 [8, 2048], P('layer', 'tok'), may hold values from -3 to 3
- dec_weight: bfloat16 [8, 8, 2048, 4096], P('layer', None, 'tok'), may hold values from -0.09375 to 0.09375
Outputs:
- rebuilt: bfloat16 [8, 1024, 4096], P('layer', 'tok')
- dec_grad: bfloat16 [8, 8, 2048, 4096], P('layer', None, 'tok')
- enc_grad: bfloat16 [8, 2048, 4096], P('layer', 'tok')
The draws below stay inside these ranges and needn't reach their ends.
All inputs are finite; a program needn't handle non-finite values.
Results may differ from the reference program's by a relative error of at most 0.022.
Values may be sent and summed in bfloat16 or wider, within the bound.
No kernel may reach another device: no remote copies, remote signals or barrier semaphores. Data moves between devices by JAX's collectives and lax.ppermute only.
A program may use at most 128 MiB of HBM per device.

```python
import math
import jax
import jax.numpy as jnp
from jax import lax

D = 4096
F = 2048
LAYERS = 8
TOKENS = 1024
N_TOK = 32


def levels(own_key, extent, cuts, smallest, largest):
    gain = 1.0
    for dim, parts in cuts:
        heights = jax.random.uniform(jax.random.fold_in(jax.random.fold_in(own_key, 6), dim), (parts,), jnp.float32, smallest / len(cuts), largest / len(cuts))
        gain = gain * jnp.repeat(jnp.exp(heights), extent[dim] // parts).reshape((-1,) + (1,) * (len(extent) - 1 - dim))
    return gain


def gaussian(key, extent, width, limit, shards=(), kind=jnp.bfloat16):
    values = jax.random.normal(key, extent, jnp.float32) * width
    if len(shards) > 0:
        values = levels(key, extent, shards, -0.22, 0.18) * values
    return jnp.clip(values, min=-limit, max=limit).astype(kind)


def setup_inputs(seed: int = 0) -> dict:
    seeds = jax.random.split(jax.random.key(seed), 6)
    acts = gaussian(seeds[0], (LAYERS, TOKENS, D), 1.0, 6.0, ((0, 8), (1, 32)))
    targets = gaussian(seeds[1], (LAYERS, TOKENS, D), 1.0, 6.0, ((0, 8), (1, 32)))
    enc_weight = gaussian(seeds[2], (LAYERS, F, D), D ** -0.5, 0.09375, ((0, 8), (1, 32)))
    enc_bias = gaussian(seeds[3], (LAYERS, F), 0.5, 3.0, ((0, 8), (1, 32)), jnp.float32)
    dec_weight = gaussian(seeds[4], (LAYERS, LAYERS, F, D), (2 * F) ** -0.5, 0.09375, ((0, 8), (2, 32)))
    return {"acts": acts, "targets": targets, "enc_weight": enc_weight, "enc_bias": enc_bias, "dec_weight": dec_weight}


def reference(acts, targets, enc_weight, enc_bias, dec_weight):
    grad_scale = 1.0 / math.sqrt(TOKENS)
    group_rows = F // N_TOK
    pre_acts = jnp.einsum('lnd,lfd->lfn', acts.astype(jnp.float32), enc_weight.astype(jnp.float32)) + enc_bias[:, :, None]
    latents = jnp.maximum(pre_acts, 0.0).astype(jnp.bfloat16)
    flat_latents = latents.reshape(LAYERS * F, TOKENS)
    layer_ids = jnp.arange(LAYERS, dtype=jnp.int32)
    rebuilt_list = []
    grad_list = []
    back_sum = jnp.zeros((LAYERS * F, TOKENS), jnp.float32)
    for target in range(LAYERS):
        keep_rows = jnp.repeat(layer_ids <= target, F)
        blocks = dec_weight[target].reshape(LAYERS * F, D)
        used = jnp.where(keep_rows[:, None], flat_latents, jnp.zeros_like(flat_latents))
        used_groups = used.reshape(LAYERS, N_TOK, group_rows, TOKENS)
        block_groups = dec_weight[target].reshape(LAYERS, N_TOK, group_rows, D)

        def add_group(group, running):
            lat_part = lax.dynamic_index_in_dim(used_groups, group, 1, keepdims=False).reshape(LAYERS * group_rows, TOKENS)
            dec_part = lax.dynamic_index_in_dim(block_groups, group, 1, keepdims=False).reshape(LAYERS * group_rows, D)
            part = lax.dot_general(lat_part, dec_part, (((0,), (0,)), ((), ())), preferred_element_type=jnp.float32)
            rounded = lax.optimization_barrier(part.astype(jnp.bfloat16))
            return running + rounded.astype(jnp.float32)
        recon_sum = lax.fori_loop(0, N_TOK, add_group, jnp.zeros((TOKENS, D), jnp.float32))
        rebuilt_list.append(recon_sum.astype(jnp.bfloat16))
        errors = (recon_sum - targets[target].astype(jnp.float32)).astype(jnp.bfloat16)
        block_grad = grad_scale * jnp.dot(flat_latents, errors, preferred_element_type=jnp.float32)
        block_grad = jnp.where(keep_rows[:, None], block_grad, 0.0)
        grad_list.append(block_grad.astype(jnp.bfloat16).reshape(LAYERS, F, D))
        grad_term = grad_scale * lax.dot_general(blocks, errors, (((1,), (1,)), ((), ())), preferred_element_type=jnp.float32)
        back_sum = back_sum + jnp.where(keep_rows[:, None], grad_term, 0.0)
    latent_grad = back_sum.reshape(LAYERS, F, TOKENS)
    pre_grad = jnp.where(pre_acts > 0, latent_grad, 0.0).astype(jnp.bfloat16)
    enc_grad = jnp.einsum('lfn,lnd->lfd', pre_grad.astype(jnp.float32), acts.astype(jnp.float32)).astype(jnp.bfloat16)
    return (jnp.stack(rebuilt_list), jnp.stack(grad_list), enc_grad)
```

```python
import math

import jax
import jax.numpy as jnp
from jax import lax
from jax.sharding import PartitionSpec as P

BF = jnp.bfloat16
F32 = jnp.float32
SIDE = 4
ORDER = (
    (
        (("x", 1), ("x", 3), ("y", 1), ("y", 3)),
        (("x", 3), ("x", 1), ("y", 3), ("y", 1)),
    ),
    (
        (("y", 1), ("y", 3), ("x", 1), ("x", 3)),
        (("y", 3), ("y", 1), ("x", 3), ("x", 1)),
    ),
)


def tok_index(x, y, core):
    return (x * SIDE + y) * 2 + core


def chip_pairs(chunk, step):
    pairs = []
    for x in range(SIDE):
        for y in range(SIDE):
            for core in range(2):
                axis, mask = ORDER[chunk][core][step]
                px, py = (x ^ mask, y) if axis == "x" else (x, y ^ mask)
                pairs.append((tok_index(x, y, core), tok_index(px, py, core)))
    return pairs


CORE_PAIRS = [(i, i ^ 1) for i in range(2 * SIDE * SIDE)]


def exchange(value, chunk, step):
    return lax.ppermute(value, "tok", chip_pairs(chunk, step))


def swap_cores(value):
    return lax.ppermute(value, "tok", CORE_PAIRS)


def dot(a, b, ca, cb):
    return lax.dot_general(a, b, (((ca,), (cb,)), ((), ())), preferred_element_type=F32)


def per_device(acts, targets, enc_weight, enc_bias, dec_weight):
    layers = lax.axis_size("layer")
    layer = lax.axis_index("layer")
    own_tokens, width = acts.shape[1:]
    tokens_all = own_tokens * lax.axis_size("tok")
    grad_scale = 1.0 / math.sqrt(tokens_all)
    rows = enc_weight.shape[1]
    part = own_tokens // 2
    chunks = range(2)

    enc = jnp.concatenate([enc_weight[0], swap_cores(enc_weight[0])], axis=0)
    bias = jnp.concatenate([enc_bias[0], swap_cores(enc_bias[0])], axis=0)
    dec = jnp.concatenate([dec_weight[0], swap_cores(dec_weight[0])], axis=1)
    both = 2 * rows
    dec_flat = dec.reshape(layers * both, width)

    acts_parts, masks, sources = [], [], []
    for c in chunks:
        near = acts[0, c * part : (c + 1) * part]
        for step in range(3):
            near = jnp.concatenate([near, exchange(near, c, step)], axis=0)
        far = exchange(near, c, 3)
        acts_parts += [near, far]
        pre = jnp.concatenate([dot(enc, near, 1, 1), dot(enc, far, 1, 1)], axis=1) + bias[:, None]
        masks.append(pre > 0)
        latents = jnp.maximum(pre, 0.0).astype(BF)
        lat_all = jnp.zeros((layers,) + latents.shape, BF)
        for hop in range(layers):
            got = latents
            if hop:
                got = lax.ppermute(latents, "layer", [(i, i + hop) for i in range(layers - hop)])
            lat_all = lax.dynamic_update_index_in_dim(
                lat_all, got, lax.rem(layer - hop + layers, layers), 0
            )
        sources.append(lat_all.reshape(layers * both, latents.shape[1]))

    rebuilt, errors = [], []
    for c in chunks:
        lat = sources[c]
        span = lat.shape[1]
        send = dot(lat[:, span // 2 :], dec_flat, 0, 0).astype(BF)
        got = exchange(send, c, 3)
        keep = dot(lat[:, : span // 2], dec_flat, 0, 0).astype(BF)
        span //= 2
        total = keep.astype(F32) + got.astype(F32)
        got = exchange(total[span // 2 :].astype(BF), c, 2)
        span //= 2
        total = total[:span] + got.astype(F32)
        target = targets[0, c * part : (c + 1) * part].astype(F32)
        for step in (1, 0):
            payload = jnp.concatenate([total[:part] - target, total[part:]], axis=0)
            got = exchange(payload.astype(BF), c, step).astype(F32)
            half = part << step
            got = got.reshape(-1, 2, half, width)[:, ::-1].reshape(span, width)
            total = total.astype(BF).astype(F32) + got
        rebuilt.append(total[:part].astype(BF))
        near = jnp.concatenate([total[:part] - target, total[part:]], axis=0).astype(BF)
        near = jnp.concatenate([near, exchange(near, c, 2)], axis=0)
        far = exchange(near, c, 3)
        errors.append((near, far))

    pre_grads = []
    for c in chunks:
        near, far = errors[c]
        partial = jnp.concatenate([dot(dec_flat, near, 1, 1), dot(dec_flat, far, 1, 1)], axis=1)
        partial = (grad_scale * partial).astype(BF).reshape(layers, both, -1)
        grad = lax.dynamic_index_in_dim(partial, layer, 0, keepdims=False).astype(F32)
        for hop in range(1, layers):
            block = lax.dynamic_index_in_dim(
                partial, lax.rem(layer - hop + layers, layers), 0, keepdims=False
            )
            got = lax.ppermute(block, "layer", [(i, i - hop) for i in range(hop, layers)])
            grad = grad + got.astype(F32)
        pre_grads.append(jnp.where(masks[c], grad, 0.0).astype(BF))

    all_errors = jnp.concatenate([e for pair in errors for e in pair], axis=0)
    all_latents = jnp.concatenate(sources, axis=1).reshape(layers, both, -1)
    own_lat = all_latents[:, :rows].reshape(layers * rows, -1)
    other_lat = all_latents[:, rows:].reshape(layers * rows, -1)
    other = (grad_scale * dot(other_lat, all_errors, 1, 0)).astype(BF)
    got = swap_cores(other)
    own = grad_scale * dot(own_lat, all_errors, 1, 0)
    dec_grad = (own + got.astype(F32)).astype(BF).reshape(layers, rows, width)

    all_acts = jnp.concatenate(acts_parts, axis=0)
    pre_grad = jnp.concatenate(pre_grads, axis=1)
    other = dot(pre_grad[rows:], all_acts, 1, 0).astype(BF)
    got = swap_cores(other)
    own = dot(pre_grad[:rows], all_acts, 1, 0)
    enc_grad = (own + got.astype(F32)).astype(BF)
    return (jnp.concatenate(rebuilt, axis=0)[None], dec_grad[None], enc_grad[None])


def solution(mesh):
    return jax.shard_map(
        per_device,
        mesh=mesh,
        in_specs=(
            P("layer", "tok", None),
            P("layer", "tok", None),
            P("layer", "tok", None),
            P("layer", "tok"),
            P("layer", None, "tok", None),
        ),
        out_specs=(P("layer", "tok", None), P("layer", None, "tok", None), P("layer", "tok", None)),
        check_vma=False,
    )
```

```python
import functools
import math

import jax
import jax.numpy as jnp
from jax import lax
from jax.experimental import pallas as pl
from jax.experimental.pallas import tpu as pltpu
from jax.sharding import PartitionSpec as P

BF = jnp.bfloat16
F32 = jnp.float32
SIDE = 4
VMEM_LIMIT = 16 * 1024 * 1024
MASKS = ((1, 3), (3, 1))
AXES = (("x", "y"), ("y", "x"))


def tok_index(x, y, core):
    return (x * SIDE + y) * 2 + core


def chip_pairs(axis, which):
    pairs = []
    for x in range(SIDE):
        for y in range(SIDE):
            for core in range(2):
                mask = MASKS[core][which]
                px, py = (x ^ mask, y) if axis == "x" else (x, y ^ mask)
                pairs.append((tok_index(x, y, core), tok_index(px, py, core)))
    return pairs


CORE_PAIRS = [(i, i ^ 1) for i in range(2 * SIDE * SIDE)]


def exchange(value, axis, which):
    return lax.ppermute(value, "tok", chip_pairs(axis, which))


def swap_cores(value):
    return lax.ppermute(value, "tok", CORE_PAIRS)


def dot(a, b, ca, cb):
    return lax.dot_general(a, b, (((ca,), (cb,)), ((), ())), preferred_element_type=F32)


def tie(*values):
    return list(lax.optimization_barrier(values))


def params():
    return pltpu.CompilerParams(vmem_limit_bytes=VMEM_LIMIT)


def cost(flops, nbytes):
    return pl.CostEstimate(flops=flops, bytes_accessed=nbytes, transcendentals=0)


def recon_body(start, layer_ref, lat_ref, own_dec, other_dec, *refs):
    outs, (own_ref, other_ref) = refs[:-2], refs[-2:]
    layers, _, both = lat_ref.shape
    tokens = own_ref.shape[0]
    half = both // 2
    block = outs[0].shape[1]

    @pl.when(pl.program_id(0) == 0)
    def _():
        for k, ref in enumerate((own_ref, other_ref)):
            pieces = []
            for s in range(layers):
                piece = lat_ref[s, start : start + tokens, k * half : (k + 1) * half]
                pieces.append(jnp.where(s <= layer_ref[0], piece, jnp.zeros_like(piece)))
            ref[...] = jnp.concatenate(pieces, axis=1)

    columns = pl.ds(pl.multiple_of(pl.program_id(0) * block, block), block)
    part = jnp.dot(own_ref[...], own_dec[:, columns], preferred_element_type=F32)
    part += jnp.dot(other_ref[...], other_dec[:, columns], preferred_element_type=F32)
    part = part.astype(BF)
    rows = outs[0].shape[0]
    for i, out in enumerate(outs):
        out[...] = part[i * rows : (i + 1) * rows]


def recon(layer, latents, start, tokens, decs, streams=4, block=2048):
    depth, width = decs[0].shape
    rows = tokens // streams
    column = lambda i, layer_ref: (0, i)
    whole = lambda i, layer_ref: (0, 0)
    return pl.pallas_call(
        functools.partial(recon_body, start),
        grid_spec=pltpu.PrefetchScalarGridSpec(
            num_scalar_prefetch=1,
            grid=(width // block,),
            in_specs=[pl.BlockSpec(memory_space=pltpu.VMEM)] * 3,
            out_specs=[pl.BlockSpec((rows, block), column)] * streams
            + [pl.BlockSpec((tokens, depth), whole)] * 2,
        ),
        out_shape=[jax.ShapeDtypeStruct((rows, width), BF)] * streams
        + [jax.ShapeDtypeStruct((tokens, depth), BF)] * 2,
        compiler_params=params(),
        cost_estimate=cost(4 * tokens * depth * width, 4 * depth * width),
    )(layer, latents, *decs)


def grads_body(scale, layer_ref, own_dec, other_dec, *refs):
    errs, refs = refs[:4], refs[4:]
    before, (out, err_ref), totals = refs[:-4], refs[-4:-2], refs[-2:]
    layers, both, _ = out.shape
    half = both // 2
    tokens, block = err_ref.shape
    at = out.shape[2] - tokens

    @pl.when(pl.program_id(0) == 0)
    def _():
        for total in totals:
            total[...] = jnp.zeros_like(total)

    err = jnp.concatenate([e[...] for e in errs], axis=0)
    err_ref[...] = err
    columns = pl.ds(pl.multiple_of(pl.program_id(0) * block, block), block)
    for total, dec in zip(totals, (own_dec, other_dec)):
        total[...] += dot(dec[:, columns], err, 1, 1)

    @pl.when(pl.program_id(0) == pl.num_programs(0) - 1)
    def _():
        for s in range(layers):
            for k, total in enumerate(totals):
                value = scale * total[s * half : (s + 1) * half, :]
                value = jnp.where(s <= layer_ref[0], value, 0.0)
                out[s, k * half : (k + 1) * half, at:] = value.astype(BF)
        for ref in before:
            out[:, :, :at] = ref[...]


def latent_grads(layer, decs, errs, before, scale, layers, block=2048):
    depth, width = decs[0].shape
    rows = errs[0].shape[0]
    tokens = rows * len(errs)
    both = 2 * depth // layers
    span = tokens + sum(b.shape[2] for b in before)
    column = lambda i, layer_ref: (0, i)
    return pl.pallas_call(
        functools.partial(grads_body, scale),
        grid_spec=pltpu.PrefetchScalarGridSpec(
            num_scalar_prefetch=1,
            grid=(width // block,),
            in_specs=[pl.BlockSpec(memory_space=pltpu.VMEM)] * 2
            + [pl.BlockSpec((rows, block), column)] * len(errs)
            + [pl.BlockSpec(memory_space=pltpu.VMEM)] * len(before),
            out_specs=[
                pl.BlockSpec((layers, both, span), lambda i, layer_ref: (0, 0, 0)),
                pl.BlockSpec((tokens, block), column),
            ],
            scratch_shapes=[pltpu.VMEM((depth, tokens), F32)] * 2,
        ),
        out_shape=[
            jax.ShapeDtypeStruct((layers, both, span), BF),
            jax.ShapeDtypeStruct((tokens, width), BF),
        ],
        compiler_params=params(),
        cost_estimate=cost(4 * tokens * depth * width, 4 * depth * width),
    )(layer, *decs, *errs, *before)


def encode_body(*refs):
    blocks, (own, other, bias, latents, mask, tokens, total) = refs[:-7], refs[-7:]

    @pl.when(pl.program_id(0) == 0)
    def _():
        total[...] = jnp.zeros_like(total)

    value = jnp.concatenate([b[...] for b in blocks], axis=0)
    tokens[...] = value
    total[...] += dot(value, jnp.concatenate([own[...], other[...]], axis=0), 1, 1)

    @pl.when(pl.program_id(0) == pl.num_programs(0) - 1)
    def _():
        pre = total[...] + bias[...]
        latents[...] = jnp.maximum(pre, 0.0).astype(BF)
        mask[...] = jnp.where(pre > 0, 1.0, 0.0).T.astype(BF)


def encode(blocks, encs, bias, block=1024):
    rows, width = blocks[0].shape
    count = rows * len(blocks)
    both = bias.shape[1]
    column = lambda i: (0, i)
    whole = lambda i: (0, 0)
    return pl.pallas_call(
        encode_body,
        grid=(width // block,),
        in_specs=[pl.BlockSpec((rows, block), column)] * len(blocks)
        + [pl.BlockSpec((both // 2, block), column)] * 2
        + [pl.BlockSpec((1, both), whole)],
        out_specs=[
            pl.BlockSpec((count, both), whole),
            pl.BlockSpec((both, count), whole),
            pl.BlockSpec((count, block), column),
        ],
        out_shape=[
            jax.ShapeDtypeStruct((count, both), BF),
            jax.ShapeDtypeStruct((both, count), BF),
            jax.ShapeDtypeStruct((count, width), BF),
        ],
        scratch_shapes=[pltpu.VMEM((count, both), F32)],
        compiler_params=params(),
        cost_estimate=cost(2 * count * both * width, 4 * count * width),
    )(*blocks, *encs, bias)


def dec_grad_body(scale, *refs):
    lats, errs, out = refs[:4], refs[4:8], refs[8]
    total = dot(lats[0][...], errs[0][...], 0, 0)
    for lat, err in zip(lats[1:], errs[1:]):
        total += dot(lat[...], err[...], 0, 0)
    out[...] = (scale * total).astype(BF)


def dec_grads(lats, errs, scale, block=1024):
    tokens, depth = lats[0].shape
    width = errs[0].shape[1]
    return pl.pallas_call(
        functools.partial(dec_grad_body, scale),
        grid=(width // block,),
        in_specs=[pl.BlockSpec((tokens, depth), lambda i: (0, 0))] * 4
        + [pl.BlockSpec((tokens, block), lambda i: (0, i))] * 4,
        out_specs=pl.BlockSpec((depth, block), lambda i: (0, i)),
        out_shape=jax.ShapeDtypeStruct((depth, width), BF),
        compiler_params=params(),
        cost_estimate=cost(8 * tokens * depth * width, 8 * tokens * width + 2 * depth * width),
    )(*lats, *errs)


def vmem_call(body, outs, *operands):
    spec = pl.BlockSpec(memory_space=pltpu.VMEM)
    return pl.pallas_call(
        body,
        in_specs=[spec] * len(operands),
        out_specs=[spec] * len(outs),
        out_shape=[jax.ShapeDtypeStruct(shape, dtype) for shape, dtype in outs],
        compiler_params=params(),
        cost_estimate=cost(
            sum(o.size for o in operands), sum(o.size * o.dtype.itemsize for o in operands)
        ),
    )(*operands)


def add_half_body(*refs):
    keep, got, send, rest = refs[:4], refs[4:8], refs[8:12], refs[12:16]
    for k, g, s, r in zip(keep, got, send, rest):
        total = k[...].astype(F32) + g[...].astype(F32)
        span = s.shape[0]
        s[...] = total[span:].astype(BF)
        r[...] = total[:span]


ORDERS = ((1, 0, 3, 2), (2, 3, 0, 1))


def group_step(turn, totals, values, target, sends):
    part = target.shape[0] // 2
    wide = sends[0].shape[1]
    for c in range(2):
        for h in range(2):
            at = slice(h * wide, (h + 1) * wide)
            value = values(c, h, at)
            totals[c][:, at] = value
            own = target[c * part : (c + 1) * part, at].astype(F32)
            for i, b in enumerate(ORDERS[h ^ turn]):
                block = value[b * part : (b + 1) * part]
                if b == 0:
                    block = block - own
                sends[2 * c + h][i * part : (i + 1) * part, :] = block.astype(BF)


def add_last_body(*refs):
    rest, got, target, totals, sends = refs[:4], refs[4:8], refs[8], refs[9:11], refs[11:15]

    def values(c, h, at):
        pieces = [rest[2 * c + j][:, at] + got[2 * c + j][:, at].astype(F32) for j in range(2)]
        return jnp.concatenate(pieces, axis=0)

    group_step(1, totals, values, target, sends)


def add_group_body(*refs):
    before, got, target, totals, sends = refs[:2], refs[2:6], refs[6], refs[7:9], refs[9:13]
    values = lambda c, h, at: before[c][:, at] + got[2 * c + h][...].astype(F32)
    group_step(0, totals, values, target, sends)


def finish_body(*refs):
    before, got, target, rebuilt, halves = refs[:2], refs[2:6], refs[6], refs[7], refs[8:12]
    part = target.shape[0] // 2
    wide = got[0].shape[1]
    for c in range(2):
        rows = slice(c * part, (c + 1) * part)
        for h in range(2):
            at = slice(h * wide, (h + 1) * wide)
            value = before[c][:, at] + got[2 * c + h][...].astype(F32)
            rebuilt[rows, at] = value[:part].astype(BF)
            for i in range(4):
                block = value[i * part : (i + 1) * part]
                if i == 0:
                    block = block - target[rows, at].astype(F32)
                where = slice((i % 2) * part, (i % 2 + 1) * part)
                halves[2 * c + i // 2][where, at] = block.astype(BF)


def per_device(acts, targets, enc_weight, enc_bias, dec_weight):
    layers = lax.axis_size("layer")
    layer_arr = lax.axis_index("layer").astype(jnp.int32).reshape(1)
    own_tokens, width = acts.shape[1:]
    tokens_all = own_tokens * lax.axis_size("tok")
    grad_scale = 1.0 / math.sqrt(tokens_all)
    rows = enc_weight.shape[1]
    both = 2 * rows
    part = own_tokens // 2
    chunks = range(2)
    streams = [(c, j) for c in chunks for j in range(2)]
    first = lambda c, j: (AXES[c][1], j)
    second = lambda c, j: (AXES[c][1], 1 - j)

    def gather_across(halves):
        got = [exchange(h, *first(c, j)) for h, (c, j) in zip(halves, streams)]
        near = tie(*[jnp.concatenate([h, g], axis=0) for h, g in zip(halves, got)])
        far = [exchange(n, *second(c, j)) for n, (c, j) in zip(near, streams)]
        return near, far

    def along_layers(value):
        return lax.all_to_all(value, "layer", 0, 0, tiled=True)

    group = [acts[0, c * part : (c + 1) * part] for c in chunks]
    bias = jnp.concatenate([enc_bias, swap_cores(enc_bias)], axis=1)
    got = [exchange(group[c], AXES[c][0], 0) for c in chunks]
    group = [jnp.concatenate([group[c], got[c]], axis=0) for c in chunks]
    got = [exchange(group[c], AXES[c][0], 1) for c in chunks]
    halves = [(group, got)[j][c] for c, j in streams]
    *halves, enc_own, dec_own = tie(*halves, enc_weight[0], dec_weight[0])
    encs = [enc_own, swap_cores(enc_own)]
    decs = [dec_own.reshape(layers * rows, width)]
    decs.append(swap_cores(decs[0]))
    near, far = gather_across(halves)

    near_latents, near_mask, near_acts = encode(near, encs, bias)
    *far, near_latents = tie(*far, near_latents)
    far_latents, far_mask, far_acts = encode(far, encs, bias)
    latents = jnp.concatenate([near_latents, far_latents], axis=0)
    all_latents = along_layers(jnp.broadcast_to(latents, (layers,) + latents.shape))
    span = near_latents.shape[0]

    *send, far_own, far_other = recon(layer_arr, all_latents, span, span, decs)
    got = [exchange(s, *second(c, j)) for s, (c, j) in zip(send, streams)]
    *keep, near_own, near_other = recon(layer_arr, all_latents, 0, span, decs)
    half = ((2 * part, width), BF)
    sums = ((2 * part, width), F32)
    *send_rest, = vmem_call(add_half_body, [half] * 4 + [sums] * 4, *keep, *got)
    send, rest = send_rest[:4], send_rest[4:]
    got = [exchange(s, *first(c, j)) for s, (c, j) in zip(send, streams)]
    target = targets[0]
    group_outs = [((4 * part, width), F32)] * 2 + [((4 * part, width // 2), BF)] * 4
    *sends, = vmem_call(add_last_body, group_outs, *rest, *got, target)
    for turn, body in ((1, add_group_body), (0, finish_body)):
        total, sends = sends[:2], sends[2:]
        got = [exchange(s, AXES[i // 2][0], (i % 2) ^ turn) for i, s in enumerate(sends)]
        outs = group_outs if turn else [((own_tokens, width), BF)] + [half] * 4
        *sends, = vmem_call(body, outs, *total, *got, target)
    rebuilt, *halves = sends
    near, far = gather_across(halves)

    near_partial, near_err = latent_grads(layer_arr, decs, near, [], grad_scale, layers)
    *far, near_partial = tie(*far, near_partial)
    partial, far_err = latent_grads(layer_arr, decs, far, [near_partial], grad_scale, layers)
    grad = along_layers(partial)

    lats = [near_own, far_own, swap_cores(near_other), swap_cores(far_other)]
    errs = [near_err, far_err, swap_cores(near_err), swap_cores(far_err)]
    dec_grad = dec_grads(lats, errs, grad_scale).reshape(layers, rows, width)

    mask = jnp.concatenate([near_mask, far_mask], axis=1).astype(F32)
    grad = (jnp.sum(grad.astype(F32), axis=0) * mask).astype(BF)
    near_grad, far_grad = grad[:, :span], grad[:, span:]

    def enc_part(which):
        return dot(near_grad[which], near_acts, 1, 0) + dot(far_grad[which], far_acts, 1, 0)

    got = swap_cores(enc_part(slice(rows, None)).astype(BF))
    enc_grad = (enc_part(slice(0, rows)) + got.astype(F32)).astype(BF)
    return (rebuilt[None], dec_grad[None], enc_grad[None])


def solution(mesh):
    return jax.shard_map(
        per_device,
        mesh=mesh,
        in_specs=(
            P("layer", "tok", None),
            P("layer", "tok", None),
            P("layer", "tok", None),
            P("layer", "tok"),
            P("layer", None, "tok", None),
        ),
        out_specs=(P("layer", "tok", None), P("layer", None, "tok", None), P("layer", "tok", None)),
        check_vma=False,
    )
```

```python
import functools
import math

import jax
import jax.numpy as jnp
from jax import lax
from jax.experimental import pallas as pl
from jax.experimental.pallas import tpu as pltpu
from jax.sharding import PartitionSpec as P

BF = jnp.bfloat16
F32 = jnp.float32
SIDE = 4
VMEM_LIMIT = 16 * 1024 * 1024
MASKS = ((3, 1), (1, 3))
AXES = (("x", "y"), ("y", "x"))


def tok_index(x, y, core):
    return (x * SIDE + y) * 2 + core


def chip_pairs(axis, which):
    pairs = []
    for x in range(SIDE):
        for y in range(SIDE):
            for core in range(2):
                mask = MASKS[core][which]
                px, py = (x ^ mask, y) if axis == "x" else (x, y ^ mask)
                pairs.append((tok_index(x, y, core), tok_index(px, py, core)))
    return pairs


CORE_PAIRS = [(i, i ^ 1) for i in range(2 * SIDE * SIDE)]


def exchange(value, axis, which):
    return lax.ppermute(value, "tok", chip_pairs(axis, which))


def swap_cores(value):
    return lax.ppermute(value, "tok", CORE_PAIRS)


def dot(a, b, ca, cb):
    return lax.dot_general(a, b, (((ca,), (cb,)), ((), ())), preferred_element_type=F32)


def tie(*values):
    return list(lax.optimization_barrier(values))


def params():
    return pltpu.CompilerParams(vmem_limit_bytes=VMEM_LIMIT)


def cost(flops, nbytes):
    return pl.CostEstimate(flops=flops, bytes_accessed=nbytes, transcendentals=0)


def recon_body(start, layer_ref, lat_ref, own_dec, other_dec, *refs):
    outs, (own_ref, other_ref) = refs[:-2], refs[-2:]
    layers, _, both = lat_ref.shape
    tokens = own_ref.shape[0]
    half = both // 2
    block = outs[0].shape[1]

    @pl.when(pl.program_id(0) == 0)
    def _():
        for k, ref in enumerate((own_ref, other_ref)):
            pieces = []
            for s in range(layers):
                piece = lat_ref[s, start : start + tokens, k * half : (k + 1) * half]
                pieces.append(jnp.where(s <= layer_ref[0], piece, jnp.zeros_like(piece)))
            ref[...] = jnp.concatenate(pieces, axis=1)

    columns = pl.ds(pl.multiple_of(pl.program_id(0) * block, block), block)
    part = jnp.dot(own_ref[...], own_dec[...], preferred_element_type=F32)
    part += jnp.dot(other_ref[...], other_dec[:, columns], preferred_element_type=F32)
    part = part.astype(BF)
    rows = outs[0].shape[0]
    for i, out in enumerate(outs):
        out[...] = part[i * rows : (i + 1) * rows]


def recon(layer, latents, start, tokens, decs, streams=2, block=1024):
    depth, width = decs[0].shape
    rows = tokens // streams
    column = lambda i, layer_ref: (0, i)
    whole = lambda i, layer_ref: (0, 0)
    return pl.pallas_call(
        functools.partial(recon_body, start),
        grid_spec=pltpu.PrefetchScalarGridSpec(
            num_scalar_prefetch=1,
            grid=(width // block,),
            in_specs=[
                pl.BlockSpec(memory_space=pltpu.VMEM),
                pl.BlockSpec((depth, block), column),
                pl.BlockSpec(memory_space=pltpu.VMEM),
            ],
            out_specs=[pl.BlockSpec((rows, block), column)] * streams
            + [pl.BlockSpec((tokens, depth), whole)] * 2,
        ),
        out_shape=[jax.ShapeDtypeStruct((rows, width), BF)] * streams
        + [jax.ShapeDtypeStruct((tokens, depth), BF)] * 2,
        compiler_params=params(),
        cost_estimate=cost(4 * tokens * depth * width, 4 * depth * width),
    )(layer, latents, *decs)


def grads_body(scale, layer_ref, own_dec, other_dec, *refs):
    errs, refs = refs[:2], refs[2:]
    before, (out, err_ref), totals = refs[:-4], refs[-4:-2], refs[-2:]
    layers, both, _ = out.shape
    half = both // 2
    tokens, block = err_ref.shape
    at = out.shape[2] - tokens

    @pl.when(pl.program_id(0) == 0)
    def _():
        for total in totals:
            total[...] = jnp.zeros_like(total)

    err = jnp.concatenate([e[...] for e in errs], axis=0)
    err_ref[...] = err
    columns = pl.ds(pl.multiple_of(pl.program_id(0) * block, block), block)
    totals[0][...] += dot(own_dec[...], err, 1, 1)
    totals[1][...] += dot(other_dec[:, columns], err, 1, 1)

    @pl.when(pl.program_id(0) == pl.num_programs(0) - 1)
    def _():
        for s in range(layers):
            for k, total in enumerate(totals):
                value = scale * total[s * half : (s + 1) * half, :]
                value = jnp.where(s <= layer_ref[0], value, 0.0)
                out[s, k * half : (k + 1) * half, at:] = value.astype(BF)
        for ref in before:
            out[:, :, :at] = ref[...]


def latent_grads(layer, decs, errs, before, scale, layers, block=1024):
    depth, width = decs[0].shape
    rows = errs[0].shape[0]
    tokens = rows * len(errs)
    both = 2 * depth // layers
    span = tokens + sum(b.shape[2] for b in before)
    column = lambda i, layer_ref: (0, i)
    return pl.pallas_call(
        functools.partial(grads_body, scale),
        grid_spec=pltpu.PrefetchScalarGridSpec(
            num_scalar_prefetch=1,
            grid=(width // block,),
            in_specs=[pl.BlockSpec((depth, block), column), pl.BlockSpec(memory_space=pltpu.VMEM)]
            + [pl.BlockSpec((rows, block), column)] * len(errs)
            + [pl.BlockSpec(memory_space=pltpu.VMEM)] * len(before),
            out_specs=[
                pl.BlockSpec((layers, both, span), lambda i, layer_ref: (0, 0, 0)),
                pl.BlockSpec((tokens, block), column),
            ],
            scratch_shapes=[pltpu.VMEM((depth, tokens), F32)] * 2,
        ),
        out_shape=[
            jax.ShapeDtypeStruct((layers, both, span), BF),
            jax.ShapeDtypeStruct((tokens, width), BF),
        ],
        compiler_params=params(),
        cost_estimate=cost(4 * tokens * depth * width, 4 * depth * width),
    )(layer, *decs, *errs, *before)


def encode_body(count, *refs):
    blocks, (own, other, bias), refs = refs[:count], refs[count : count + 3], refs[count + 3 :]
    before, (latents, mask, tokens, total) = refs[:-4], refs[-4:]

    @pl.when(pl.program_id(0) == 0)
    def _():
        total[...] = jnp.zeros_like(total)

    value = jnp.concatenate([b[...] for b in blocks], axis=0)
    tokens[...] = value
    total[...] += dot(value, jnp.concatenate([own[...], other[...]], axis=0), 1, 1)

    @pl.when(pl.program_id(0) == pl.num_programs(0) - 1)
    def _():
        pre = total[...] + bias[...]
        value = jnp.maximum(pre, 0.0).astype(BF)
        mask[...] = jnp.where(pre > 0, 1.0, 0.0).T.astype(BF)
        if before:
            at = before[0].shape[0]
            for i in range(latents.shape[0]):
                latents[i, :at, :] = before[0][...]
                latents[i, at:, :] = value
        else:
            latents[...] = value


def encode(blocks, encs, bias, before=(), layers=0, block=1024):
    rows, width = blocks[0].shape
    count = rows * len(blocks)
    both = bias.shape[1]
    column = lambda i: (0, i)
    whole = lambda i: (0, 0)
    if before:
        shape = (layers, before[0].shape[0] + count, both)
        spec = pl.BlockSpec(shape, lambda i: (0, 0, 0))
    else:
        shape = (count, both)
        spec = pl.BlockSpec(shape, whole)
    return pl.pallas_call(
        functools.partial(encode_body, len(blocks)),
        grid=(width // block,),
        in_specs=[pl.BlockSpec((rows, block), column)] * len(blocks)
        + [pl.BlockSpec((both // 2, block), column)] * 2
        + [pl.BlockSpec((1, both), whole)]
        + [pl.BlockSpec(b.shape, whole) for b in before],
        out_specs=[
            spec,
            pl.BlockSpec((both, count), whole),
            pl.BlockSpec((count, block), column),
        ],
        out_shape=[
            jax.ShapeDtypeStruct(shape, BF),
            jax.ShapeDtypeStruct((both, count), BF),
            jax.ShapeDtypeStruct((count, width), BF),
        ],
        scratch_shapes=[pltpu.VMEM((count, both), F32)],
        compiler_params=params(),
        cost_estimate=cost(2 * count * both * width, 4 * count * width),
    )(*blocks, *encs, bias, *before)


def dec_grad_body(scale, *refs):
    lats, errs, out = refs[:4], refs[4:8], refs[8]
    total = dot(lats[0][...], errs[0][...], 0, 0)
    for lat, err in zip(lats[1:], errs[1:]):
        total += dot(lat[...], err[...], 0, 0)
    out[...] = (scale * total).astype(BF)


def dec_grads(lats, errs, scale, block=1024):
    tokens, depth = lats[0].shape
    width = errs[0].shape[1]
    return pl.pallas_call(
        functools.partial(dec_grad_body, scale),
        grid=(width // block,),
        in_specs=[pl.BlockSpec((tokens, depth), lambda i: (0, 0))] * 4
        + [pl.BlockSpec((tokens, block), lambda i: (0, i))] * 4,
        out_specs=pl.BlockSpec((depth, block), lambda i: (0, i)),
        out_shape=jax.ShapeDtypeStruct((depth, width), BF),
        compiler_params=params(),
        cost_estimate=cost(8 * tokens * depth * width, 8 * tokens * width + 2 * depth * width),
    )(*lats, *errs)


def vmem_call(body, outs, *operands):
    spec = pl.BlockSpec(memory_space=pltpu.VMEM)
    return pl.pallas_call(
        body,
        in_specs=[spec] * len(operands),
        out_specs=[spec] * len(outs),
        out_shape=[jax.ShapeDtypeStruct(shape, dtype) for shape, dtype in outs],
        compiler_params=params(),
        cost_estimate=cost(
            sum(o.size for o in operands), sum(o.size * o.dtype.itemsize for o in operands)
        ),
    )(*operands)


def add_half_body(*refs):
    keep, got, send, rest = refs[:2], refs[2:4], refs[4:6], refs[6:8]
    for k, g, s, r in zip(keep, got, send, rest):
        total = k[...].astype(F32) + g[...].astype(F32)
        span = s.shape[0]
        s[...] = total[span:].astype(BF)
        r[...] = total[:span]


ORDERS = ((1, 0, 3, 2), (2, 3, 0, 1))


def group_body(which, *refs):
    before, got, target, totals, sends = refs[:2], refs[2:4], refs[4], refs[5:7], refs[7:9]
    part = target.shape[0] // 2
    for c in range(2):
        value = before[c][...] + got[c][...].astype(F32)
        totals[c][...] = value
        own = target[c * part : (c + 1) * part, :].astype(F32)
        for i, b in enumerate(ORDERS[which]):
            block = value[b * part : (b + 1) * part]
            if b == 0:
                block = block - own
            sends[c][i * part : (i + 1) * part, :] = block.astype(BF)


def finish_body(*refs):
    before, got, target, rebuilt, errs = refs[:2], refs[2:4], refs[4], refs[5], refs[6:8]
    part = target.shape[0] // 2
    for c in range(2):
        rows = slice(c * part, (c + 1) * part)
        value = before[c][...] + got[c][...].astype(F32)
        rebuilt[rows, :] = value[:part].astype(BF)
        own = value[:part] - target[rows, :].astype(F32)
        errs[c][...] = jnp.concatenate([own, value[part:]], axis=0).astype(BF)


def per_device(acts, targets, enc_weight, enc_bias, dec_weight):
    layers = lax.axis_size("layer")
    layer_arr = lax.axis_index("layer").astype(jnp.int32).reshape(1)
    own_tokens, width = acts.shape[1:]
    tokens_all = own_tokens * lax.axis_size("tok")
    grad_scale = 1.0 / math.sqrt(tokens_all)
    rows = enc_weight.shape[1]
    part = own_tokens // 2
    chunks = range(2)

    def in_group(values, which):
        return [exchange(v, AXES[c][0], which) for c, v in zip(chunks, values)]

    def across(values, which):
        return [exchange(v, AXES[c][1], which) for c, v in zip(chunks, values)]

    def join(values, others):
        return [jnp.concatenate(pair, axis=0) for pair in zip(values, others)]

    group = [acts[0, c * part : (c + 1) * part] for c in chunks]
    bias = jnp.concatenate([enc_bias, swap_cores(enc_bias)], axis=1)
    group = join(group, in_group(group, 0))
    group = join(group, in_group(group, 1))
    *group, enc_own = tie(*group, enc_weight[0])
    encs = [enc_own, swap_cores(enc_own)]
    near = join(group, across(group, 0))
    *near, dec_own = tie(*near, dec_weight[0])
    decs = [dec_own.reshape(layers * rows, width)]
    decs.append(swap_cores(decs[0]))
    far = across(near, 1)

    def along_layers(value):
        return lax.all_to_all(value, "layer", 0, 0, tiled=True)

    near_latents, near_mask, near_acts = encode(near, encs, bias)
    *far, near_latents = tie(*far, near_latents)
    latents, far_mask, far_acts = encode(far, encs, bias, [near_latents], layers)
    latents = along_layers(latents)
    span = near_latents.shape[0]

    *send, far_own, far_other = recon(layer_arr, latents, span, span, decs)
    far_swapped = swap_cores(far_other)
    send, far_swapped = tie(send, far_swapped)
    got = across(send, 1)
    *keep, near_own, near_other = recon(layer_arr, latents, 0, span, decs)
    target = targets[0]
    half = ((4 * part, width), BF)
    sums = ((4 * part, width), F32)
    out = vmem_call(add_half_body, [half] * 2 + [sums] * 2, *keep, *got)
    others = [swap_cores(near_other), far_swapped]
    body = lambda which: functools.partial(group_body, which)
    out = vmem_call(body(1), [sums] * 2 + [half] * 2, *out[2:], *across(out[:2], 0), target)
    out = vmem_call(body(0), [sums] * 2 + [half] * 2, *out[:2], *in_group(out[2:], 1), target)
    outs = [((own_tokens, width), BF)] + [half] * 2
    rebuilt, *errs = vmem_call(finish_body, outs, *out[:2], *in_group(out[2:], 0), target)
    near = tie(*join(errs, across(errs, 0)))
    far = across(near, 1)

    near_partial, near_err = latent_grads(layer_arr, decs, near, [], grad_scale, layers)
    far, near_partial, near_err = tie(far, near_partial, near_err)
    partial, far_err = latent_grads(layer_arr, decs, far, [near_partial], grad_scale, layers)
    grad = along_layers(partial)

    lats = [near_own, others[0], far_own, others[1]]
    errs = [near_err, swap_cores(near_err), far_err, swap_cores(far_err)]
    dec_grad = dec_grads(lats, errs, grad_scale).reshape(layers, rows, width)
    grad, dec_grad = tie(grad, dec_grad)

    mask = jnp.concatenate([near_mask, far_mask], axis=1).astype(F32)
    grad = (jnp.sum(grad.astype(F32), axis=0) * mask).astype(BF)
    near_grad, far_grad = grad[:, :span], grad[:, span:]

    def enc_part(which):
        return dot(near_grad[which], near_acts, 1, 0) + dot(far_grad[which], far_acts, 1, 0)

    got = swap_cores(enc_part(slice(rows, None)).astype(BF))
    enc_grad = (enc_part(slice(0, rows)) + got.astype(F32)).astype(BF)
    return (rebuilt[None], dec_grad[None], enc_grad[None])


def solution(mesh):
    return jax.shard_map(
        per_device,
        mesh=mesh,
        in_specs=(
            P("layer", "tok", None),
            P("layer", "tok", None),
            P("layer", "tok", None),
            P("layer", "tok"),
            P("layer", None, "tok", None),
        ),
        out_specs=(P("layer", "tok", None), P("layer", None, "tok", None), P("layer", "tok", None)),
        check_vma=False,
    )
```

```python
import functools
import math

import jax
import jax.numpy as jnp
from jax import lax
from jax.experimental import pallas as pl
from jax.experimental.pallas import tpu as pltpu
from jax.sharding import PartitionSpec as P

BF = jnp.bfloat16
F32 = jnp.float32
SIDE = 4
VMEM_LIMIT = 16 * 1024 * 1024
MASKS = ((3, 1), (1, 3))
AXES = (("x", "y"), ("y", "x"))


def tok_index(x, y, core):
    return (x * SIDE + y) * 2 + core


def chip_pairs(axis, which):
    pairs = []
    for x in range(SIDE):
        for y in range(SIDE):
            for core in range(2):
                mask = MASKS[core][which]
                px, py = (x ^ mask, y) if axis == "x" else (x, y ^ mask)
                pairs.append((tok_index(x, y, core), tok_index(px, py, core)))
    return pairs


CORE_PAIRS = [(i, i ^ 1) for i in range(2 * SIDE * SIDE)]


def exchange(value, axis, which):
    return lax.ppermute(value, "tok", chip_pairs(axis, which))


def swap_cores(value):
    return lax.ppermute(value, "tok", CORE_PAIRS)


def dot(a, b, ca, cb):
    return lax.dot_general(a, b, (((ca,), (cb,)), ((), ())), preferred_element_type=F32)


def tie(*values):
    return list(lax.optimization_barrier(values))


def params():
    return pltpu.CompilerParams(vmem_limit_bytes=VMEM_LIMIT)


def cost(flops, nbytes):
    return pl.CostEstimate(flops=flops, bytes_accessed=nbytes, transcendentals=0)


def recon_body(start, layer_ref, lat_ref, own_dec, other_dec, *refs):
    outs, (own_ref, other_ref) = refs[:-2], refs[-2:]
    layers, _, both = lat_ref.shape
    tokens = own_ref.shape[0]
    half = both // 2

    @pl.when(pl.program_id(0) == 0)
    def _():
        for k, ref in enumerate((own_ref, other_ref)):
            pieces = []
            for s in range(layers):
                piece = lat_ref[s, start : start + tokens, k * half : (k + 1) * half]
                pieces.append(jnp.where(s <= layer_ref[0], piece, jnp.zeros_like(piece)))
            ref[...] = jnp.concatenate(pieces, axis=1)

    part = jnp.dot(own_ref[...], own_dec[...], preferred_element_type=F32)
    part += jnp.dot(other_ref[...], other_dec[...], preferred_element_type=F32)
    part = part.astype(BF)
    rows = outs[0].shape[0]
    for i, out in enumerate(outs):
        out[...] = part[i * rows : (i + 1) * rows]


def recon(layer, latents, start, tokens, decs, streams, block=1024):
    depth, width = decs[0].shape
    rows = tokens // streams
    column = lambda i, layer_ref: (0, i)
    whole = lambda i, layer_ref: (0, 0)
    return pl.pallas_call(
        functools.partial(recon_body, start),
        grid_spec=pltpu.PrefetchScalarGridSpec(
            num_scalar_prefetch=1,
            grid=(width // block,),
            in_specs=[pl.BlockSpec(memory_space=pltpu.VMEM)]
            + [pl.BlockSpec((depth, block), column)] * 2,
            out_specs=[pl.BlockSpec((rows, block), column)] * streams
            + [pl.BlockSpec((tokens, depth), whole)] * 2,
        ),
        out_shape=[jax.ShapeDtypeStruct((rows, width), BF)] * streams
        + [jax.ShapeDtypeStruct((tokens, depth), BF)] * 2,
        compiler_params=params(),
        cost_estimate=cost(4 * tokens * depth * width, 4 * depth * width),
    )(layer, latents, *decs)


def grads_body(scale, count, layer_ref, own_dec, other_dec, *refs):
    errs, refs = refs[:count], refs[count:]
    before, (out, err_ref), totals = refs[:-4], refs[-4:-2], refs[-2:]
    layers, both, _ = out.shape
    half = both // 2
    tokens = err_ref.shape[0]
    at = out.shape[2] - tokens

    @pl.when(pl.program_id(0) == 0)
    def _():
        for total in totals:
            total[...] = jnp.zeros_like(total)

    err = jnp.concatenate([e[...] for e in errs], axis=0)
    err_ref[...] = err
    totals[0][...] += dot(own_dec[...], err, 1, 1)
    totals[1][...] += dot(other_dec[...], err, 1, 1)

    @pl.when(pl.program_id(0) == pl.num_programs(0) - 1)
    def _():
        for s in range(layers):
            for k, total in enumerate(totals):
                value = scale * total[s * half : (s + 1) * half, :]
                value = jnp.where(s <= layer_ref[0], value, 0.0)
                out[s, k * half : (k + 1) * half, at:] = value.astype(BF)
        for ref in before:
            out[:, :, :at] = ref[...]


def latent_grads(layer, decs, errs, before, scale, layers, block=1024):
    depth, width = decs[0].shape
    rows = errs[0].shape[0]
    tokens = rows * len(errs)
    both = 2 * depth // layers
    span = tokens + sum(b.shape[2] for b in before)
    column = lambda i, layer_ref: (0, i)
    return pl.pallas_call(
        functools.partial(grads_body, scale, len(errs)),
        grid_spec=pltpu.PrefetchScalarGridSpec(
            num_scalar_prefetch=1,
            grid=(width // block,),
            in_specs=[pl.BlockSpec((depth, block), column)] * 2
            + [pl.BlockSpec((rows, block), column)] * len(errs)
            + [pl.BlockSpec(memory_space=pltpu.VMEM)] * len(before),
            out_specs=[
                pl.BlockSpec((layers, both, span), lambda i, layer_ref: (0, 0, 0)),
                pl.BlockSpec((tokens, block), column),
            ],
            scratch_shapes=[pltpu.VMEM((depth, tokens), F32)] * 2,
        ),
        out_shape=[
            jax.ShapeDtypeStruct((layers, both, span), BF),
            jax.ShapeDtypeStruct((tokens, width), BF),
        ],
        compiler_params=params(),
        cost_estimate=cost(4 * tokens * depth * width, 4 * depth * width),
    )(layer, *decs, *errs, *before)


def encode_body(count, *refs):
    blocks, (own, other, bias), refs = refs[:count], refs[count : count + 3], refs[count + 3 :]
    before, (latents, mask, tokens, total) = refs[:-4], refs[-4:]

    @pl.when(pl.program_id(0) == 0)
    def _():
        total[...] = jnp.zeros_like(total)

    value = jnp.concatenate([b[...] for b in blocks], axis=0)
    tokens[...] = value
    total[...] += dot(value, jnp.concatenate([own[...], other[...]], axis=0), 1, 1)

    @pl.when(pl.program_id(0) == pl.num_programs(0) - 1)
    def _():
        pre = total[...] + bias[...]
        value = jnp.maximum(pre, 0.0).astype(BF)
        mask[...] = jnp.where(pre > 0, 1.0, 0.0).T.astype(BF)
        if before:
            at = before[0].shape[0]
            for i in range(latents.shape[0]):
                latents[i, :at, :] = before[0][...]
                latents[i, at:, :] = value
        else:
            latents[...] = value


def encode(blocks, encs, bias, before=(), layers=0, block=1024):
    rows, width = blocks[0].shape
    count = rows * len(blocks)
    both = bias.shape[1]
    column = lambda i: (0, i)
    whole = lambda i: (0, 0)
    if before:
        shape = (layers, before[0].shape[0] + count, both)
        spec = pl.BlockSpec(shape, lambda i: (0, 0, 0))
    else:
        shape = (count, both)
        spec = pl.BlockSpec(shape, whole)
    return pl.pallas_call(
        functools.partial(encode_body, len(blocks)),
        grid=(width // block,),
        in_specs=[pl.BlockSpec((rows, block), column)] * len(blocks)
        + [pl.BlockSpec((both // 2, block), column)] * 2
        + [pl.BlockSpec((1, both), whole)]
        + [pl.BlockSpec(b.shape, whole) for b in before],
        out_specs=[
            spec,
            pl.BlockSpec((both, count), whole),
            pl.BlockSpec((count, block), column),
        ],
        out_shape=[
            jax.ShapeDtypeStruct(shape, BF),
            jax.ShapeDtypeStruct((both, count), BF),
            jax.ShapeDtypeStruct((count, width), BF),
        ],
        scratch_shapes=[pltpu.VMEM((count, both), F32)],
        compiler_params=params(),
        cost_estimate=cost(2 * count * both * width, 4 * count * width),
    )(*blocks, *encs, bias, *before)


def dec_grad_body(scale, *refs):
    lats, errs, out = refs[:4], refs[4:8], refs[8]
    total = dot(lats[0][...], errs[0][...], 0, 0)
    for lat, err in zip(lats[1:], errs[1:]):
        total += dot(lat[...], err[...], 0, 0)
    out[...] = (scale * total).astype(BF)


def dec_grads(lats, errs, scale, block=1024):
    tokens = sum(lat.shape[0] for lat in lats) // 4
    depth, width = lats[0].shape[1], errs[0].shape[1]
    return pl.pallas_call(
        functools.partial(dec_grad_body, scale),
        grid=(width // block,),
        in_specs=[pl.BlockSpec(lat.shape, lambda i: (0, 0)) for lat in lats]
        + [pl.BlockSpec((err.shape[0], block), lambda i: (0, i)) for err in errs],
        out_specs=pl.BlockSpec((depth, block), lambda i: (0, i)),
        out_shape=jax.ShapeDtypeStruct((depth, width), BF),
        compiler_params=params(),
        cost_estimate=cost(8 * tokens * depth * width, 8 * tokens * width + 2 * depth * width),
    )(*lats, *errs)


def vmem_call(body, outs, *operands):
    spec = pl.BlockSpec(memory_space=pltpu.VMEM)
    return pl.pallas_call(
        body,
        in_specs=[spec] * len(operands),
        out_specs=[spec] * len(outs),
        out_shape=[jax.ShapeDtypeStruct(shape, dtype) for shape, dtype in outs],
        compiler_params=params(),
        cost_estimate=cost(
            sum(o.size for o in operands), sum(o.size * o.dtype.itemsize for o in operands)
        ),
    )(*operands)


def add_body(*refs):
    count = len(refs) // 3
    for a, b, out in zip(refs[:count], refs[count : 2 * count], refs[2 * count :]):
        out[...] = (a[...].astype(F32) + b[...].astype(F32)).astype(out.dtype)


ORDERS = ((1, 0, 3, 2), (2, 3, 0, 1))


def group_body(which, *refs):
    terms, (target, *outs) = refs[:-5], refs[-5:]
    totals, sends = outs[:2], outs[2:]
    part = target.shape[0] // 2
    for c in range(2):
        value = sum(t[...].astype(F32) for t in terms[c::2])
        totals[c][...] = value
        own = target[c * part : (c + 1) * part, :].astype(F32)
        for i, b in enumerate(ORDERS[which]):
            block = value[b * part : (b + 1) * part]
            if b == 0:
                block = block - own
            sends[c][i * part : (i + 1) * part, :] = block.astype(BF)


def finish_body(*refs):
    before, got, target, rebuilt, errs = refs[:2], refs[2:4], refs[4], refs[5], refs[6:8]
    part = target.shape[0] // 2
    for c in range(2):
        rows = slice(c * part, (c + 1) * part)
        value = before[c][...] + got[c][...].astype(F32)
        rebuilt[rows, :] = value[:part].astype(BF)
        own = value[:part] - target[rows, :].astype(F32)
        errs[c][...] = jnp.concatenate([own, value[part:]], axis=0).astype(BF)


def per_device(acts, targets, enc_weight, enc_bias, dec_weight):
    layers = lax.axis_size("layer")
    layer_arr = lax.axis_index("layer").astype(jnp.int32).reshape(1)
    own_tokens, width = acts.shape[1:]
    tokens_all = own_tokens * lax.axis_size("tok")
    grad_scale = 1.0 / math.sqrt(tokens_all)
    rows = enc_weight.shape[1]
    part = own_tokens // 2
    chunks = range(2)

    def in_group(values, which):
        return [exchange(v, AXES[c][0], which) for c, v in zip(chunks, values)]

    def across(values, which):
        return [exchange(v, AXES[c][1], which) for c, v in zip(chunks, values)]

    def join(values, others):
        return [jnp.concatenate(pair, axis=0) for pair in zip(values, others)]

    group = [acts[0, c * part : (c + 1) * part] for c in chunks]
    bias = jnp.concatenate([enc_bias, swap_cores(enc_bias)], axis=1)
    group = join(group, in_group(group, 0))
    group = join(group, in_group(group, 1))
    *group, enc_own, dec_own = tie(*group, enc_weight[0], dec_weight[0])
    encs = [enc_own, swap_cores(enc_own)]
    decs = [dec_own.reshape(layers * rows, width)]

    def spread(group):
        direct = across(group, 0)
        early = [*group, *direct, *across(group, 1)]
        return early, across(direct, 1)

    early, late = spread(group)
    *early, dec_own = tie(*early, decs[0])
    decs.append(swap_cores(dec_own))

    def along_layers(value):
        return lax.all_to_all(value, "layer", 0, 0, tiled=True)

    early_latents, early_mask, early_acts = encode(early, encs, bias)
    *late, early_latents = tie(*late, early_latents)
    latents, late_mask, late_acts = encode(late, encs, bias, [early_latents], layers)
    latents = along_layers(latents)
    span, count = early_latents.shape[0], late_mask.shape[1]

    *send, late_own, late_other = recon(layer_arr, latents, span, count, decs, 2)
    late_swapped = swap_cores(late_other)
    send, late_swapped = tie(send, late_swapped)
    got = across(send, 1)
    *parts, early_own, early_other = recon(layer_arr, latents, 0, span, decs, 6)
    others = [swap_cores(early_other), late_swapped]
    target = targets[0]
    half = ((4 * part, width), BF)
    sums = ((4 * part, width), F32)
    send = vmem_call(add_body, [half] * 2, *parts[2:4], *got)
    got = across(send, 0) + across(parts[4:], 1)
    body = lambda which: functools.partial(group_body, which)
    out = vmem_call(body(1), [sums] * 2 + [half] * 2, *parts[:2], *got, target)
    out = vmem_call(body(0), [sums] * 2 + [half] * 2, *out[:2], *in_group(out[2:], 1), target)
    outs = [((own_tokens, width), BF)] + [half] * 2
    rebuilt, *errs = vmem_call(finish_body, outs, *out[:2], *in_group(out[2:], 0), target)
    early, late = spread(errs)
    partial, early_err = latent_grads(layer_arr, decs, early, [], grad_scale, layers)
    late, partial, early_err = tie(late, partial, early_err)
    partial, late_err = latent_grads(layer_arr, decs, late, [partial], grad_scale, layers)
    grad = along_layers(partial)

    lats = [early_own, others[0], late_own, others[1]]
    errs = [early_err, swap_cores(early_err), late_err, swap_cores(late_err)]
    dec_grad = dec_grads(lats, errs, grad_scale).reshape(layers, rows, width)
    grad, dec_grad = tie(grad, dec_grad)

    mask = jnp.concatenate([early_mask, late_mask], axis=1).astype(F32)
    grad = (jnp.sum(grad.astype(F32), axis=0) * mask).astype(BF)
    early_grad, late_grad = grad[:, :span], grad[:, span:]

    def enc_part(which):
        return dot(early_grad[which], early_acts, 1, 0) + dot(late_grad[which], late_acts, 1, 0)

    got = swap_cores(enc_part(slice(rows, None)).astype(BF))
    enc_grad = (enc_part(slice(0, rows)) + got.astype(F32)).astype(BF)
    return (rebuilt[None], dec_grad[None], enc_grad[None])


def solution(mesh):
    return jax.shard_map(
        per_device,
        mesh=mesh,
        in_specs=(
            P("layer", "tok", None),
            P("layer", "tok", None),
            P("layer", "tok", None),
            P("layer", "tok"),
            P("layer", None, "tok", None),
        ),
        out_specs=(P("layer", "tok", None), P("layer", None, "tok", None), P("layer", "tok", None)),
        check_vma=False,
    )
```

```python
import functools
import math

import jax
import jax.numpy as jnp
from jax import lax
from jax.experimental import pallas as pl
from jax.experimental.pallas import tpu as pltpu
from jax.sharding import PartitionSpec as P

BF = jnp.bfloat16
F32 = jnp.float32
SIDE = 4
VMEM_LIMIT = 16 * 1024 * 1024
MASKS = ((3, 1), (1, 3))
AXES = (("x", "y"), ("y", "x"))


def tok_index(x, y, core):
    return (x * SIDE + y) * 2 + core


def chip_pairs(axis, which):
    pairs = []
    for x in range(SIDE):
        for y in range(SIDE):
            for core in range(2):
                mask = MASKS[core][which]
                px, py = (x ^ mask, y) if axis == "x" else (x, y ^ mask)
                pairs.append((tok_index(x, y, core), tok_index(px, py, core)))
    return pairs


CORE_PAIRS = [(i, i ^ 1) for i in range(2 * SIDE * SIDE)]


def exchange(value, axis, which):
    return lax.ppermute(value, "tok", chip_pairs(axis, which))


def swap_cores(value):
    return lax.ppermute(value, "tok", CORE_PAIRS)


def dot(a, b, ca, cb):
    return lax.dot_general(a, b, (((ca,), (cb,)), ((), ())), preferred_element_type=F32)


def tie(*values):
    return list(lax.optimization_barrier(values))


def params():
    return pltpu.CompilerParams(vmem_limit_bytes=VMEM_LIMIT)


def cost(flops, nbytes):
    return pl.CostEstimate(flops=flops, bytes_accessed=nbytes, transcendentals=0)


def recon_body(start, layer_ref, *refs):
    hops, (own_dec, other_dec), refs = refs[:8], refs[8:10], refs[10:]
    outs, (own_ref, other_ref, all_ref) = refs[:-3], refs[-3:]
    layers, both = len(hops), hops[0].shape[1]
    half = both // 2
    tokens = all_ref.shape[0]

    @pl.when(pl.program_id(0) == 0)
    def _():
        for hop in range(layers):
            source = lax.rem(layer_ref[0] - hop + layers, layers)
            at = pl.ds(pl.multiple_of(source * both, both), both)
            piece = hops[hop][start : start + tokens, :]
            all_ref[:, at] = jnp.where(hop <= layer_ref[0], piece, jnp.zeros_like(piece))
        lat = all_ref[...]
        for k, ref in enumerate((own_ref, other_ref)):
            pieces = [lat[:, (2 * s + k) * half : (2 * s + k + 1) * half] for s in range(layers)]
            ref[...] = jnp.concatenate(pieces, axis=1)

    part = jnp.dot(own_ref[...], own_dec[...], preferred_element_type=F32)
    part += jnp.dot(other_ref[...], other_dec[...], preferred_element_type=F32)
    part = part.astype(BF)
    rows = outs[0].shape[0]
    for i, out in enumerate(outs):
        out[...] = part[i * rows : (i + 1) * rows]


def recon(layer, hops, start, tokens, decs, streams, block=1024):
    depth, width = decs[0].shape
    both = hops[0].shape[1]
    rows = tokens // streams
    column = lambda i, layer_ref: (0, i)
    whole = lambda i, layer_ref: (0, 0)
    return pl.pallas_call(
        functools.partial(recon_body, start),
        grid_spec=pltpu.PrefetchScalarGridSpec(
            num_scalar_prefetch=1,
            grid=(width // block,),
            in_specs=[pl.BlockSpec(memory_space=pltpu.VMEM)] * len(hops)
            + [pl.BlockSpec((depth, block), column)] * 2,
            out_specs=[pl.BlockSpec((rows, block), column)] * streams
            + [pl.BlockSpec((tokens, depth), whole)] * 2,
            scratch_shapes=[pltpu.VMEM((tokens, 2 * depth), BF)],
        ),
        out_shape=[jax.ShapeDtypeStruct((rows, width), BF)] * streams
        + [jax.ShapeDtypeStruct((tokens, depth), BF)] * 2,
        compiler_params=params(),
        cost_estimate=cost(4 * tokens * depth * width, 4 * depth * width),
    )(layer, *hops, *decs)


def grads_body(scale, layers, count, layer_ref, own_dec, other_dec, *refs):
    errs, refs = refs[:count], refs[count:]
    before, outs, (err_ref, *totals) = refs[: -3 - layers], refs[-3 - layers : -3], refs[-3:]
    half = outs[0].shape[0] // 2
    tokens = err_ref.shape[0]
    at = outs[0].shape[1] - tokens

    @pl.when(pl.program_id(0) == 0)
    def _():
        for total in totals:
            total[...] = jnp.zeros_like(total)

    err = jnp.concatenate([e[...] for e in errs], axis=0)
    err_ref[...] = err
    for total, dec in zip(totals, (own_dec, other_dec)):
        total[...] += dot(dec[...], err, 1, 1)

    @pl.when(pl.program_id(0) == pl.num_programs(0) - 1)
    def _():
        for hop, out in enumerate(outs):
            source = lax.rem(layer_ref[0] - hop + layers, layers)
            where = pl.ds(pl.multiple_of(source * half, half), half)
            for k, total in enumerate(totals):
                value = jnp.where(hop <= layer_ref[0], scale * total[where, :], 0.0)
                out[k * half : (k + 1) * half, at:] = value.astype(BF)
        for ref, out in zip(before, outs):
            out[:, :at] = ref[...]


def latent_grads(layer, decs, errs, before, scale, layers, block=1024):
    depth, width = decs[0].shape
    rows = errs[0].shape[0]
    tokens = rows * len(errs)
    both = 2 * depth // layers
    span = tokens + (before[0].shape[1] if before else 0)
    column = lambda i, layer_ref: (0, i)
    whole = lambda i, layer_ref: (0, 0)
    return pl.pallas_call(
        functools.partial(grads_body, scale, layers, len(errs)),
        grid_spec=pltpu.PrefetchScalarGridSpec(
            num_scalar_prefetch=1,
            grid=(width // block,),
            in_specs=[pl.BlockSpec((depth, block), column)] * 2
            + [pl.BlockSpec((rows, block), column)] * len(errs)
            + [pl.BlockSpec(memory_space=pltpu.VMEM)] * len(before),
            out_specs=[pl.BlockSpec((both, span), whole)] * layers
            + [pl.BlockSpec((tokens, block), column)],
            scratch_shapes=[pltpu.VMEM((depth, tokens), F32)] * 2,
        ),
        out_shape=[jax.ShapeDtypeStruct((both, span), BF)] * layers
        + [jax.ShapeDtypeStruct((tokens, width), BF)],
        compiler_params=params(),
        cost_estimate=cost(4 * tokens * depth * width, 4 * depth * width),
    )(layer, *decs, *errs, *before)


def encode_body(count, *refs):
    blocks, (own, other, bias), refs = refs[:count], refs[count : count + 3], refs[count + 3 :]
    before, (latents, mask, tokens, total) = refs[:-4], refs[-4:]

    @pl.when(pl.program_id(0) == 0)
    def _():
        total[...] = jnp.zeros_like(total)

    value = jnp.concatenate([b[...] for b in blocks], axis=0)
    tokens[...] = value
    total[...] += dot(value, jnp.concatenate([own[...], other[...]], axis=0), 1, 1)

    @pl.when(pl.program_id(0) == pl.num_programs(0) - 1)
    def _():
        pre = total[...] + bias[...]
        value = jnp.maximum(pre, 0.0).astype(BF)
        mask[...] = jnp.where(pre > 0, 1.0, 0.0).T.astype(BF)
        at = latents.shape[0] - value.shape[0]
        latents[at:, :] = value
        for ref in before:
            latents[:at, :] = ref[...]


def encode(blocks, encs, bias, before=(), block=1024):
    rows, width = blocks[0].shape
    count = rows * len(blocks)
    both = bias.shape[1]
    column = lambda i: (0, i)
    whole = lambda i: (0, 0)
    span = count + sum(b.shape[0] for b in before)
    return pl.pallas_call(
        functools.partial(encode_body, len(blocks)),
        grid=(width // block,),
        in_specs=[pl.BlockSpec((rows, block), column)] * len(blocks)
        + [pl.BlockSpec((both // 2, block), column)] * 2
        + [pl.BlockSpec((1, both), whole)]
        + [pl.BlockSpec(b.shape, whole) for b in before],
        out_specs=[
            pl.BlockSpec((span, both), whole),
            pl.BlockSpec((both, count), whole),
            pl.BlockSpec((count, block), column),
        ],
        out_shape=[
            jax.ShapeDtypeStruct((span, both), BF),
            jax.ShapeDtypeStruct((both, count), BF),
            jax.ShapeDtypeStruct((count, width), BF),
        ],
        scratch_shapes=[pltpu.VMEM((count, both), F32)],
        compiler_params=params(),
        cost_estimate=cost(2 * count * both * width, 4 * count * width),
    )(*blocks, *encs, bias, *before)


def dec_grad_body(scale, *refs):
    lats, errs, out = refs[:4], refs[4:8], refs[8]
    total = dot(lats[0][...], errs[0][...], 0, 0)
    for lat, err in zip(lats[1:], errs[1:]):
        total += dot(lat[...], err[...], 0, 0)
    out[...] = (scale * total).astype(BF)


def dec_grads(lats, errs, scale, block=1024):
    tokens = sum(lat.shape[0] for lat in lats) // 4
    depth, width = lats[0].shape[1], errs[0].shape[1]
    return pl.pallas_call(
        functools.partial(dec_grad_body, scale),
        grid=(width // block,),
        in_specs=[pl.BlockSpec(lat.shape, lambda i: (0, 0)) for lat in lats]
        + [pl.BlockSpec((err.shape[0], block), lambda i: (0, i)) for err in errs],
        out_specs=pl.BlockSpec((depth, block), lambda i: (0, i)),
        out_shape=jax.ShapeDtypeStruct((depth, width), BF),
        compiler_params=params(),
        cost_estimate=cost(8 * tokens * depth * width, 8 * tokens * width + 2 * depth * width),
    )(*lats, *errs)


def vmem_call(body, outs, *operands):
    spec = pl.BlockSpec(memory_space=pltpu.VMEM)
    return pl.pallas_call(
        body,
        in_specs=[spec] * len(operands),
        out_specs=[spec] * len(outs),
        out_shape=[jax.ShapeDtypeStruct(shape, dtype) for shape, dtype in outs],
        compiler_params=params(),
        cost_estimate=cost(
            sum(o.size for o in operands), sum(o.size * o.dtype.itemsize for o in operands)
        ),
    )(*operands)


def add_body(*refs):
    count = len(refs) // 3
    for a, b, out in zip(refs[:count], refs[count : 2 * count], refs[2 * count :]):
        out[...] = (a[...].astype(F32) + b[...].astype(F32)).astype(out.dtype)


ORDERS = ((1, 0, 3, 2), (2, 3, 0, 1))


def group_body(which, *refs):
    terms, (target, *outs) = refs[:-5], refs[-5:]
    totals, sends = outs[:2], outs[2:]
    part = target.shape[0] // 2
    for c in range(2):
        value = sum(t[...].astype(F32) for t in terms[c::2])
        totals[c][...] = value
        own = target[c * part : (c + 1) * part, :].astype(F32)
        for i, b in enumerate(ORDERS[which]):
            block = value[b * part : (b + 1) * part]
            if b == 0:
                block = block - own
            sends[c][i * part : (i + 1) * part, :] = block.astype(BF)


def finish_body(*refs):
    before, got, target, rebuilt, errs = refs[:2], refs[2:4], refs[4], refs[5], refs[6:8]
    part = target.shape[0] // 2
    for c in range(2):
        rows = slice(c * part, (c + 1) * part)
        value = before[c][...] + got[c][...].astype(F32)
        rebuilt[rows, :] = value[:part].astype(BF)
        own = value[:part] - target[rows, :].astype(F32)
        errs[c][...] = jnp.concatenate([own, value[part:]], axis=0).astype(BF)


def per_device(acts, targets, enc_weight, enc_bias, dec_weight):
    layers = lax.axis_size("layer")
    layer_arr = lax.axis_index("layer").astype(jnp.int32).reshape(1)
    own_tokens, width = acts.shape[1:]
    tokens_all = own_tokens * lax.axis_size("tok")
    grad_scale = 1.0 / math.sqrt(tokens_all)
    rows = enc_weight.shape[1]
    part = own_tokens // 2
    chunks = range(2)

    def in_group(values, which):
        return [exchange(v, AXES[c][0], which) for c, v in zip(chunks, values)]

    def across(values, which):
        return [exchange(v, AXES[c][1], which) for c, v in zip(chunks, values)]

    def join(values, others):
        return [jnp.concatenate(pair, axis=0) for pair in zip(values, others)]

    group = [acts[0, c * part : (c + 1) * part] for c in chunks]
    bias = jnp.concatenate([enc_bias, swap_cores(enc_bias)], axis=1)
    group = join(group, in_group(group, 0))
    group = join(group, in_group(group, 1))
    *group, enc_own, dec_own = tie(*group, enc_weight[0], dec_weight[0])
    encs = [enc_own, swap_cores(enc_own)]
    decs = [dec_own.reshape(layers * rows, width)]

    def spread(group):
        direct = across(group, 0)
        early = [*group, *direct, *across(group, 1)]
        return early, across(direct, 1)

    early, late = spread(group)
    *early, dec_own = tie(*early, decs[0])
    decs.append(swap_cores(dec_own))

    def shift(value, hop, least=0):
        if hop > 0:
            pairs = [(i, i + hop) for i in range(least, layers - hop)]
        else:
            pairs = [(i, i + hop) for i in range(max(least, -hop), layers)]
        return lax.ppermute(value, "layer", pairs)

    early_latents, early_mask, early_acts = encode(early, encs, bias)
    *late, early_latents = tie(*late, early_latents)
    latents, late_mask, late_acts = encode(late, encs, bias, [early_latents])
    one, two = shift(latents, 1), shift(latents, 2)
    hops = [latents, one, two, shift(one, 2, 1), shift(two, 2, 2)]
    hops += [shift(latents, hop) for hop in range(5, layers)]
    span, count = early_latents.shape[0], late_mask.shape[1]

    *send, late_own, late_other = recon(layer_arr, hops, span, count, decs, 2)
    late_swapped = swap_cores(late_other)
    send, late_swapped = tie(send, late_swapped)
    got = across(send, 1)
    *parts, early_own, early_other = recon(layer_arr, hops, 0, span, decs, 6)
    others = [swap_cores(early_other), late_swapped]
    target = targets[0]
    half = ((4 * part, width), BF)
    sums = ((4 * part, width), F32)
    send = vmem_call(add_body, [half] * 2, *parts[2:4], *got)
    got = across(send, 0) + across(parts[4:], 1)
    body = lambda which: functools.partial(group_body, which)
    out = vmem_call(body(1), [sums] * 2 + [half] * 2, *parts[:2], *got, target)
    out = vmem_call(body(0), [sums] * 2 + [half] * 2, *out[:2], *in_group(out[2:], 1), target)
    outs = [((own_tokens, width), BF)] + [half] * 2
    rebuilt, *errs = vmem_call(finish_body, outs, *out[:2], *in_group(out[2:], 0), target)
    early, late = spread(errs)
    *hops, early_err = latent_grads(layer_arr, decs, early, [], grad_scale, layers)
    late, hops, early_err = tie(late, hops, early_err)
    *hops, late_err = latent_grads(layer_arr, decs, late, hops, grad_scale, layers)
    relayed = [shift(hops[3], -2, 3), shift(hops[4], -2, 4)]
    grads = [hops[0]] + [shift(hops[hop], -hop) for hop in range(5, layers)]
    near = vmem_call(add_body, [(h.shape, BF) for h in hops[1:3]], *hops[1:3], *relayed)
    near, errs = tie(near, [early_err, late_err])
    grads += [shift(near[0], -1), shift(near[1], -2)]

    lats = [early_own, others[0], late_own, others[1]]
    errs = [errs[0], swap_cores(errs[0]), errs[1], swap_cores(errs[1])]
    dec_grad = dec_grads(lats, errs, grad_scale).reshape(layers, rows, width)
    grads, dec_grad = tie(grads, dec_grad)

    mask = jnp.concatenate([early_mask, late_mask], axis=1).astype(F32)
    grad = (sum(g.astype(F32) for g in grads) * mask).astype(BF)
    early_grad, late_grad = grad[:, :span], grad[:, span:]

    def enc_part(which):
        return dot(early_grad[which], early_acts, 1, 0) + dot(late_grad[which], late_acts, 1, 0)

    got = swap_cores(enc_part(slice(rows, None)).astype(BF))
    enc_grad = (enc_part(slice(0, rows)) + got.astype(F32)).astype(BF)
    return (rebuilt[None], dec_grad[None], enc_grad[None])


def solution(mesh):
    return jax.shard_map(
        per_device,
        mesh=mesh,
        in_specs=(
            P("layer", "tok", None),
            P("layer", "tok", None),
            P("layer", "tok", None),
            P("layer", "tok"),
            P("layer", None, "tok", None),
        ),
        out_specs=(P("layer", "tok", None), P("layer", None, "tok", None), P("layer", "tok", None)),
        check_vma=False,
    )
```

```python
import functools
import math

import jax
import jax.numpy as jnp
from jax import lax
from jax.experimental import pallas as pl
from jax.experimental.pallas import tpu as pltpu
from jax.sharding import PartitionSpec as P

BF = jnp.bfloat16
F32 = jnp.float32
SIDE = 4
VMEM_LIMIT = 16 * 1024 * 1024
MASKS = ((3, 1), (1, 3))
AXES = (("x", "y"), ("y", "x"))


def tok_index(x, y, core):
    return (x * SIDE + y) * 2 + core


def chip_pairs(axis, which):
    pairs = []
    for x in range(SIDE):
        for y in range(SIDE):
            for core in range(2):
                mask = MASKS[core][which]
                px, py = (x ^ mask, y) if axis == "x" else (x, y ^ mask)
                pairs.append((tok_index(x, y, core), tok_index(px, py, core)))
    return pairs


CORE_PAIRS = [(i, i ^ 1) for i in range(2 * SIDE * SIDE)]


def exchange(value, axis, which):
    return lax.ppermute(value, "tok", chip_pairs(axis, which))


def swap_cores(value):
    return lax.ppermute(value, "tok", CORE_PAIRS)


def dot(a, b, ca, cb):
    return lax.dot_general(a, b, (((ca,), (cb,)), ((), ())), preferred_element_type=F32)


def tie(*values):
    return list(lax.optimization_barrier(values))


def params():
    return pltpu.CompilerParams(vmem_limit_bytes=VMEM_LIMIT)


def cost(flops, nbytes):
    return pl.CostEstimate(flops=flops, bytes_accessed=nbytes, transcendentals=0)


def recon_body(start, layer_ref, *refs):
    hops, (own_dec, other_dec), refs = refs[:8], refs[8:10], refs[10:]
    outs, (own_ref, other_ref, all_ref) = refs[:-3], refs[-3:]
    layers, both = len(hops), hops[0].shape[1]
    half = both // 2
    tokens = all_ref.shape[0]

    @pl.when(pl.program_id(0) == 0)
    def _():
        for hop in range(layers):
            source = lax.rem(layer_ref[0] - hop + layers, layers)
            at = pl.ds(pl.multiple_of(source * both, both), both)
            piece = hops[hop][start : start + tokens, :]
            all_ref[:, at] = jnp.where(hop <= layer_ref[0], piece, jnp.zeros_like(piece))
        lat = all_ref[...]
        for k, ref in enumerate((own_ref, other_ref)):
            pieces = [lat[:, (2 * s + k) * half : (2 * s + k + 1) * half] for s in range(layers)]
            ref[...] = jnp.concatenate(pieces, axis=1)

    part = jnp.dot(own_ref[...], own_dec[...], preferred_element_type=F32)
    part += jnp.dot(other_ref[...], other_dec[...], preferred_element_type=F32)
    part = part.astype(BF)
    rows = outs[0].shape[0]
    for i, out in enumerate(outs):
        out[...] = part[i * rows : (i + 1) * rows]


def recon(layer, hops, start, tokens, decs, streams, block=1024):
    depth, width = decs[0].shape
    both = hops[0].shape[1]
    rows = tokens // streams
    column = lambda i, layer_ref: (0, i)
    whole = lambda i, layer_ref: (0, 0)
    return pl.pallas_call(
        functools.partial(recon_body, start),
        grid_spec=pltpu.PrefetchScalarGridSpec(
            num_scalar_prefetch=1,
            grid=(width // block,),
            in_specs=[pl.BlockSpec(memory_space=pltpu.VMEM)] * len(hops)
            + [pl.BlockSpec((depth, block), column)] * 2,
            out_specs=[pl.BlockSpec((rows, block), column)] * streams
            + [pl.BlockSpec((tokens, depth), whole)] * 2,
            scratch_shapes=[pltpu.VMEM((tokens, 2 * depth), BF)],
        ),
        out_shape=[jax.ShapeDtypeStruct((rows, width), BF)] * streams
        + [jax.ShapeDtypeStruct((tokens, depth), BF)] * 2,
        compiler_params=params(),
        cost_estimate=cost(4 * tokens * depth * width, 4 * depth * width),
    )(layer, *hops, *decs)


def grads_body(scale, layers, count, layer_ref, own_dec, other_dec, *refs):
    errs, refs = refs[:count], refs[count:]
    before, outs, (err_ref, *totals) = refs[: -3 - layers], refs[-3 - layers : -3], refs[-3:]
    half = outs[0].shape[0] // 2
    tokens = err_ref.shape[0]
    at = outs[0].shape[1] - tokens

    @pl.when(pl.program_id(0) == 0)
    def _():
        for total in totals:
            total[...] = jnp.zeros_like(total)

    err = jnp.concatenate([e[...] for e in errs], axis=0)
    err_ref[...] = err
    for total, dec in zip(totals, (own_dec, other_dec)):
        total[...] += dot(dec[...], err, 1, 1)

    @pl.when(pl.program_id(0) == pl.num_programs(0) - 1)
    def _():
        for hop, out in enumerate(outs):
            source = lax.rem(layer_ref[0] - hop + layers, layers)
            where = pl.ds(pl.multiple_of(source * half, half), half)
            for k, total in enumerate(totals):
                value = jnp.where(hop <= layer_ref[0], scale * total[where, :], 0.0)
                out[k * half : (k + 1) * half, at:] = value.astype(BF)
        for ref, out in zip(before, outs):
            out[:, :at] = ref[...]


def latent_grads(layer, decs, errs, before, scale, layers, block=1024):
    depth, width = decs[0].shape
    rows = errs[0].shape[0]
    tokens = rows * len(errs)
    both = 2 * depth // layers
    span = tokens + (before[0].shape[1] if before else 0)
    column = lambda i, layer_ref: (0, i)
    whole = lambda i, layer_ref: (0, 0)
    return pl.pallas_call(
        functools.partial(grads_body, scale, layers, len(errs)),
        grid_spec=pltpu.PrefetchScalarGridSpec(
            num_scalar_prefetch=1,
            grid=(width // block,),
            in_specs=[pl.BlockSpec((depth, block), column)] * 2
            + [pl.BlockSpec((rows, block), column)] * len(errs)
            + [pl.BlockSpec(memory_space=pltpu.VMEM)] * len(before),
            out_specs=[pl.BlockSpec((both, span), whole)] * layers
            + [pl.BlockSpec((tokens, block), column)],
            scratch_shapes=[pltpu.VMEM((depth, tokens), F32)] * 2,
        ),
        out_shape=[jax.ShapeDtypeStruct((both, span), BF)] * layers
        + [jax.ShapeDtypeStruct((tokens, width), BF)],
        compiler_params=params(),
        cost_estimate=cost(4 * tokens * depth * width, 4 * depth * width),
    )(layer, *decs, *errs, *before)


def encode_body(count, *refs):
    blocks, (own, other, bias), refs = refs[:count], refs[count : count + 3], refs[count + 3 :]
    before, (latents, mask, tokens, total) = refs[:-4], refs[-4:]

    @pl.when(pl.program_id(0) == 0)
    def _():
        total[...] = jnp.zeros_like(total)

    value = jnp.concatenate([b[...] for b in blocks], axis=0)
    tokens[...] = value
    total[...] += dot(value, jnp.concatenate([own[...], other[...]], axis=0), 1, 1)

    @pl.when(pl.program_id(0) == pl.num_programs(0) - 1)
    def _():
        pre = total[...] + bias[...]
        value = jnp.maximum(pre, 0.0).astype(BF)
        mask[...] = jnp.where(pre > 0, 1.0, 0.0).T.astype(BF)
        at = latents.shape[0] - value.shape[0]
        latents[at:, :] = value
        for ref in before:
            latents[:at, :] = ref[...]


def encode(blocks, encs, bias, before=(), block=1024):
    rows, width = blocks[0].shape
    count = rows * len(blocks)
    both = bias.shape[1]
    column = lambda i: (0, i)
    whole = lambda i: (0, 0)
    span = count + sum(b.shape[0] for b in before)
    return pl.pallas_call(
        functools.partial(encode_body, len(blocks)),
        grid=(width // block,),
        in_specs=[pl.BlockSpec((rows, block), column)] * len(blocks)
        + [pl.BlockSpec((both // 2, block), column)] * 2
        + [pl.BlockSpec((1, both), whole)]
        + [pl.BlockSpec(b.shape, whole) for b in before],
        out_specs=[
            pl.BlockSpec((span, both), whole),
            pl.BlockSpec((both, count), whole),
            pl.BlockSpec((count, block), column),
        ],
        out_shape=[
            jax.ShapeDtypeStruct((span, both), BF),
            jax.ShapeDtypeStruct((both, count), BF),
            jax.ShapeDtypeStruct((count, width), BF),
        ],
        scratch_shapes=[pltpu.VMEM((count, both), F32)],
        compiler_params=params(),
        cost_estimate=cost(2 * count * both * width, 4 * count * width),
    )(*blocks, *encs, bias, *before)


def dec_grad_body(scale, *refs):
    lats, errs, out = refs[:4], refs[4:8], refs[8]
    total = dot(lats[0][...], errs[0][...], 0, 0)
    for lat, err in zip(lats[1:], errs[1:]):
        total += dot(lat[...], err[...], 0, 0)
    out[...] = (scale * total).astype(BF)


def dec_grads(lats, errs, scale, block=1024):
    tokens = sum(lat.shape[0] for lat in lats) // 4
    depth, width = lats[0].shape[1], errs[0].shape[1]
    return pl.pallas_call(
        functools.partial(dec_grad_body, scale),
        grid=(width // block,),
        in_specs=[pl.BlockSpec(lat.shape, lambda i: (0, 0)) for lat in lats]
        + [pl.BlockSpec((err.shape[0], block), lambda i: (0, i)) for err in errs],
        out_specs=pl.BlockSpec((depth, block), lambda i: (0, i)),
        out_shape=jax.ShapeDtypeStruct((depth, width), BF),
        compiler_params=params(),
        cost_estimate=cost(8 * tokens * depth * width, 8 * tokens * width + 2 * depth * width),
    )(*lats, *errs)


def vmem_call(body, outs, *operands):
    spec = pl.BlockSpec(memory_space=pltpu.VMEM)
    return pl.pallas_call(
        body,
        in_specs=[spec] * len(operands),
        out_specs=[spec] * len(outs),
        out_shape=[jax.ShapeDtypeStruct(shape, dtype) for shape, dtype in outs],
        compiler_params=params(),
        cost_estimate=cost(
            sum(o.size for o in operands), sum(o.size * o.dtype.itemsize for o in operands)
        ),
    )(*operands)


def add_body(*refs):
    count = len(refs) // 3
    for a, b, out in zip(refs[:count], refs[count : 2 * count], refs[2 * count :]):
        out[...] = (a[...].astype(F32) + b[...].astype(F32)).astype(out.dtype)


ORDERS = ((1, 0, 3, 2), (2, 3, 0, 1))


def group_body(which, *refs):
    terms, (target, *outs) = refs[:-5], refs[-5:]
    totals, sends = outs[:2], outs[2:]
    part = target.shape[0] // 2
    for c in range(2):
        value = sum(t[...].astype(F32) for t in terms[c::2])
        totals[c][...] = value
        own = target[c * part : (c + 1) * part, :].astype(F32)
        for i, b in enumerate(ORDERS[which]):
            block = value[b * part : (b + 1) * part]
            if b == 0:
                block = block - own
            sends[c][i * part : (i + 1) * part, :] = block.astype(BF)


def finish_body(*refs):
    before, got, target, rebuilt, errs = refs[:2], refs[2:4], refs[4], refs[5], refs[6:8]
    part = target.shape[0] // 2
    for c in range(2):
        rows = slice(c * part, (c + 1) * part)
        value = before[c][...] + got[c][...].astype(F32)
        rebuilt[rows, :] = value[:part].astype(BF)
        own = value[:part] - target[rows, :].astype(F32)
        errs[c][...] = jnp.concatenate([own, value[part:]], axis=0).astype(BF)


def per_device(acts, targets, enc_weight, enc_bias, dec_weight):
    layers = lax.axis_size("layer")
    layer_arr = lax.axis_index("layer").astype(jnp.int32).reshape(1)
    own_tokens, width = acts.shape[1:]
    tokens_all = own_tokens * lax.axis_size("tok")
    grad_scale = 1.0 / math.sqrt(tokens_all)
    rows = enc_weight.shape[1]
    part = own_tokens // 2
    chunks = range(2)

    def in_group(values, which):
        return [exchange(v, AXES[c][0], which) for c, v in zip(chunks, values)]

    def across(values, which):
        return [exchange(v, AXES[c][1], which) for c, v in zip(chunks, values)]

    def join(values, others):
        return [jnp.concatenate(pair, axis=0) for pair in zip(values, others)]

    group = [acts[0, c * part : (c + 1) * part] for c in chunks]
    group = join(group, in_group(group, 0))
    group = join(group, in_group(group, 1))
    *group, enc_own, dec_own, bias = tie(*group, enc_weight[0], dec_weight[0], enc_bias)
    encs = [enc_own, swap_cores(enc_own)]
    bias = jnp.concatenate([bias, swap_cores(bias)], axis=1)
    decs = [dec_own.reshape(layers * rows, width)]

    def spread(group):
        direct = across(group, 0)
        early = [*group, *direct, *across(group, 1)]
        return early, across(direct, 1)

    early, late = spread(group)
    *early, dec_own = tie(*early, decs[0])
    decs.append(swap_cores(dec_own))

    def shift(value, hop, least=0):
        if hop > 0:
            pairs = [(i, i + hop) for i in range(least, layers - hop)]
        else:
            pairs = [(i, i + hop) for i in range(max(least, -hop), layers)]
        return lax.ppermute(value, "layer", pairs)

    early_latents, early_mask, early_acts = encode(early, encs, bias)
    *late, early_latents = tie(*late, early_latents)
    latents, late_mask, late_acts = encode(late, encs, bias, [early_latents])
    one, two = shift(latents, 1), shift(latents, 2)
    hops = [latents, one, two, shift(one, 2, 1), shift(two, 2, 2)]
    hops += [shift(latents, hop) for hop in range(5, layers)]
    span, count = early_latents.shape[0], late_mask.shape[1]

    *send, late_own, late_other = recon(layer_arr, hops, span, count, decs, 2)
    late_swapped = swap_cores(late_other)
    send, late_swapped = tie(send, late_swapped)
    got = across(send, 1)
    *parts, early_own, early_other = recon(layer_arr, hops, 0, span, decs, 6)
    others = [swap_cores(early_other), late_swapped]
    target = targets[0]
    half = ((4 * part, width), BF)
    sums = ((4 * part, width), F32)
    send = vmem_call(add_body, [half] * 2, *parts[2:4], *got)
    got = across(send, 0) + across(parts[4:], 1)
    body = lambda which: functools.partial(group_body, which)
    out = vmem_call(body(1), [sums] * 2 + [half] * 2, *parts[:2], *got, target)
    out = vmem_call(body(0), [sums] * 2 + [half] * 2, *out[:2], *in_group(out[2:], 1), target)
    outs = [((own_tokens, width), BF)] + [half] * 2
    rebuilt, *errs = vmem_call(finish_body, outs, *out[:2], *in_group(out[2:], 0), target)
    early, late = spread(errs)
    *hops, early_err = latent_grads(layer_arr, decs, early, [], grad_scale, layers)
    late, hops, early_err = tie(late, hops, early_err)
    *hops, late_err = latent_grads(layer_arr, decs, late, hops, grad_scale, layers)
    relayed = [shift(hops[3], -2, 3), shift(hops[4], -2, 4)]
    lats = [early_own, others[0], late_own, others[1]]
    errs = [early_err, swap_cores(early_err), late_err, swap_cores(late_err)]
    dec_grad = dec_grads(lats, errs, grad_scale).reshape(layers, rows, width)
    grads = [hops[0]] + [shift(hops[hop], -hop) for hop in range(5, layers)]
    relayed, dec_grad = tie(relayed, dec_grad)
    near = vmem_call(add_body, [(h.shape, BF) for h in hops[1:3]], *hops[1:3], *relayed)
    grads += [shift(near[0], -1), shift(near[1], -2)]

    mask = jnp.concatenate([early_mask, late_mask], axis=1).astype(F32)
    grad = (sum(g.astype(F32) for g in grads) * mask).astype(BF)
    early_grad, late_grad = grad[:, :span], grad[:, span:]

    def enc_part(which):
        return dot(early_grad[which], early_acts, 1, 0) + dot(late_grad[which], late_acts, 1, 0)

    got = swap_cores(enc_part(slice(rows, None)).astype(BF))
    enc_grad = (enc_part(slice(0, rows)) + got.astype(F32)).astype(BF)
    return (rebuilt[None], dec_grad[None], enc_grad[None])


def solution(mesh):
    return jax.shard_map(
        per_device,
        mesh=mesh,
        in_specs=(
            P("layer", "tok", None),
            P("layer", "tok", None),
            P("layer", "tok", None),
            P("layer", "tok"),
            P("layer", None, "tok", None),
        ),
        out_specs=(P("layer", "tok", None), P("layer", None, "tok", None), P("layer", "tok", None)),
        check_vma=False,
    )
```

```python
import functools
import math

import jax
import jax.numpy as jnp
from jax import lax
from jax.experimental import pallas as pl
from jax.experimental.pallas import tpu as pltpu
from jax.sharding import PartitionSpec as P

BF = jnp.bfloat16
F32 = jnp.float32
SIDE = 4
VMEM_LIMIT = 16 * 1024 * 1024
MASKS = ((3, 1), (1, 3))
AXES = (("x", "y"), ("y", "x"))


def tok_index(x, y, core):
    return (x * SIDE + y) * 2 + core


def chip_pairs(axis, which):
    pairs = []
    for x in range(SIDE):
        for y in range(SIDE):
            for core in range(2):
                mask = MASKS[core][which]
                px, py = (x ^ mask, y) if axis == "x" else (x, y ^ mask)
                pairs.append((tok_index(x, y, core), tok_index(px, py, core)))
    return pairs


CORE_PAIRS = [(i, i ^ 1) for i in range(2 * SIDE * SIDE)]


def exchange(value, axis, which):
    return lax.ppermute(value, "tok", chip_pairs(axis, which))


def swap_cores(value):
    return lax.ppermute(value, "tok", CORE_PAIRS)


def dot(a, b, ca, cb):
    return lax.dot_general(a, b, (((ca,), (cb,)), ((), ())), preferred_element_type=F32)


def tie(*values):
    return list(lax.optimization_barrier(values))


def params():
    return pltpu.CompilerParams(vmem_limit_bytes=VMEM_LIMIT)


def cost(flops, nbytes):
    return pl.CostEstimate(flops=flops, bytes_accessed=nbytes, transcendentals=0)


def recon_body(start, layer_ref, *refs):
    hops, (own_dec, other_dec), refs = refs[:8], refs[8:10], refs[10:]
    outs, (own_ref, other_ref, all_ref) = refs[:-3], refs[-3:]
    layers, both = len(hops), hops[0].shape[1]
    half = both // 2
    tokens = all_ref.shape[0]

    @pl.when(pl.program_id(0) == 0)
    def _():
        for hop in range(layers):
            source = lax.rem(layer_ref[0] - hop + layers, layers)
            at = pl.ds(pl.multiple_of(source * both, both), both)
            piece = hops[hop][start : start + tokens, :]
            all_ref[:, at] = jnp.where(hop <= layer_ref[0], piece, jnp.zeros_like(piece))
        lat = all_ref[...]
        for k, ref in enumerate((own_ref, other_ref)):
            pieces = [lat[:, (2 * s + k) * half : (2 * s + k + 1) * half] for s in range(layers)]
            ref[...] = jnp.concatenate(pieces, axis=1)

    part = jnp.dot(own_ref[...], own_dec[...], preferred_element_type=F32)
    part += jnp.dot(other_ref[...], other_dec[...], preferred_element_type=F32)
    part = part.astype(BF)
    rows = outs[0].shape[0]
    for i, out in enumerate(outs):
        out[...] = part[i * rows : (i + 1) * rows]


def recon(layer, hops, start, tokens, decs, streams, block=1024):
    depth, width = decs[0].shape
    both = hops[0].shape[1]
    rows = tokens // streams
    column = lambda i, layer_ref: (0, i)
    whole = lambda i, layer_ref: (0, 0)
    return pl.pallas_call(
        functools.partial(recon_body, start),
        grid_spec=pltpu.PrefetchScalarGridSpec(
            num_scalar_prefetch=1,
            grid=(width // block,),
            in_specs=[pl.BlockSpec(memory_space=pltpu.VMEM)] * len(hops)
            + [pl.BlockSpec((depth, block), column)] * 2,
            out_specs=[pl.BlockSpec((rows, block), column)] * streams
            + [pl.BlockSpec((tokens, depth), whole)] * 2,
            scratch_shapes=[pltpu.VMEM((tokens, 2 * depth), BF)],
        ),
        out_shape=[jax.ShapeDtypeStruct((rows, width), BF)] * streams
        + [jax.ShapeDtypeStruct((tokens, depth), BF)] * 2,
        compiler_params=params(),
        cost_estimate=cost(4 * tokens * depth * width, 4 * depth * width),
    )(layer, *hops, *decs)


def grads_body(scale, layers, count, layer_ref, own_dec, other_dec, *refs):
    errs, refs = refs[:count], refs[count:]
    before, outs, (err_ref, *totals) = refs[: -3 - layers], refs[-3 - layers : -3], refs[-3:]
    half = outs[0].shape[0] // 2
    tokens = err_ref.shape[0]
    at = outs[0].shape[1] - tokens

    @pl.when(pl.program_id(0) == 0)
    def _():
        for total in totals:
            total[...] = jnp.zeros_like(total)

    err = jnp.concatenate([e[...] for e in errs], axis=0)
    err_ref[...] = err
    for total, dec in zip(totals, (own_dec, other_dec)):
        total[...] += dot(dec[...], err, 1, 1)

    @pl.when(pl.program_id(0) == pl.num_programs(0) - 1)
    def _():
        for hop, out in enumerate(outs):
            source = lax.rem(layer_ref[0] - hop + layers, layers)
            where = pl.ds(pl.multiple_of(source * half, half), half)
            for k, total in enumerate(totals):
                value = jnp.where(hop <= layer_ref[0], scale * total[where, :], 0.0)
                out[k * half : (k + 1) * half, at:] = value.astype(BF)
        for ref, out in zip(before, outs):
            out[:, :at] = ref[...]


def latent_grads(layer, decs, errs, before, scale, layers, block=1024):
    depth, width = decs[0].shape
    rows = errs[0].shape[0]
    tokens = rows * len(errs)
    both = 2 * depth // layers
    span = tokens + (before[0].shape[1] if before else 0)
    column = lambda i, layer_ref: (0, i)
    whole = lambda i, layer_ref: (0, 0)
    return pl.pallas_call(
        functools.partial(grads_body, scale, layers, len(errs)),
        grid_spec=pltpu.PrefetchScalarGridSpec(
            num_scalar_prefetch=1,
            grid=(width // block,),
            in_specs=[pl.BlockSpec((depth, block), column)] * 2
            + [pl.BlockSpec((rows, block), column)] * len(errs)
            + [pl.BlockSpec(memory_space=pltpu.VMEM)] * len(before),
            out_specs=[pl.BlockSpec((both, span), whole)] * layers
            + [pl.BlockSpec((tokens, block), column)],
            scratch_shapes=[pltpu.VMEM((depth, tokens), F32)] * 2,
        ),
        out_shape=[jax.ShapeDtypeStruct((both, span), BF)] * layers
        + [jax.ShapeDtypeStruct((tokens, width), BF)],
        compiler_params=params(),
        cost_estimate=cost(4 * tokens * depth * width, 4 * depth * width),
    )(layer, *decs, *errs, *before)


def encode_body(count, *refs):
    blocks, (own, other, bias), refs = refs[:count], refs[count : count + 3], refs[count + 3 :]
    before, (latents, mask, tokens, total) = refs[:-4], refs[-4:]

    @pl.when(pl.program_id(0) == 0)
    def _():
        total[...] = jnp.zeros_like(total)

    value = jnp.concatenate([b[...] for b in blocks], axis=0)
    tokens[...] = value
    total[...] += dot(value, jnp.concatenate([own[...], other[...]], axis=0), 1, 1)

    @pl.when(pl.program_id(0) == pl.num_programs(0) - 1)
    def _():
        pre = total[...] + bias[...]
        value = jnp.maximum(pre, 0.0).astype(BF)
        mask[...] = jnp.where(pre > 0, 1.0, 0.0).T.astype(BF)
        at = latents.shape[0] - value.shape[0]
        latents[at:, :] = value
        for ref in before:
            latents[:at, :] = ref[...]


def encode(blocks, encs, bias, before=(), block=1024):
    rows, width = blocks[0].shape
    count = rows * len(blocks)
    both = bias.shape[1]
    column = lambda i: (0, i)
    whole = lambda i: (0, 0)
    span = count + sum(b.shape[0] for b in before)
    return pl.pallas_call(
        functools.partial(encode_body, len(blocks)),
        grid=(width // block,),
        in_specs=[pl.BlockSpec((rows, block), column)] * len(blocks)
        + [pl.BlockSpec((both // 2, block), column)] * 2
        + [pl.BlockSpec((1, both), whole)]
        + [pl.BlockSpec(b.shape, whole) for b in before],
        out_specs=[
            pl.BlockSpec((span, both), whole),
            pl.BlockSpec((both, count), whole),
            pl.BlockSpec((count, block), column),
        ],
        out_shape=[
            jax.ShapeDtypeStruct((span, both), BF),
            jax.ShapeDtypeStruct((both, count), BF),
            jax.ShapeDtypeStruct((count, width), BF),
        ],
        scratch_shapes=[pltpu.VMEM((count, both), F32)],
        compiler_params=params(),
        cost_estimate=cost(2 * count * both * width, 4 * count * width),
    )(*blocks, *encs, bias, *before)


def dec_grad_body(scale, *refs):
    lats, errs, out = refs[:4], refs[4:8], refs[-1]
    total = dot(lats[0][...], errs[0][...], 0, 0)
    for lat, err in zip(lats[1:], errs[1:]):
        total += dot(lat[...], err[...], 0, 0)
    out[...] = (scale * total).astype(BF)


def dec_grads(lats, errs, scale, start, before=(), block=1024):
    tokens = sum(lat.shape[0] for lat in lats) // 4
    depth, width = lats[0].shape[1], errs[0].shape[1]
    steps = width // block // 2
    column = lambda i: (0, i + start * steps)
    return pl.pallas_call(
        functools.partial(dec_grad_body, scale),
        grid=(steps,),
        in_specs=[pl.BlockSpec(lat.shape, lambda i: (0, 0)) for lat in lats]
        + [pl.BlockSpec((err.shape[0], block), column) for err in errs]
        + [pl.BlockSpec(memory_space=pl.ANY)] * len(before),
        out_specs=pl.BlockSpec((depth, block), column),
        out_shape=jax.ShapeDtypeStruct((depth, width), BF),
        input_output_aliases={8: 0} if before else {},
        compiler_params=params(),
        cost_estimate=cost(4 * tokens * depth * width, 4 * tokens * width + depth * width),
    )(*lats, *errs, *before)


def vmem_call(body, outs, *operands):
    spec = pl.BlockSpec(memory_space=pltpu.VMEM)
    return pl.pallas_call(
        body,
        in_specs=[spec] * len(operands),
        out_specs=[spec] * len(outs),
        out_shape=[jax.ShapeDtypeStruct(shape, dtype) for shape, dtype in outs],
        compiler_params=params(),
        cost_estimate=cost(
            sum(o.size for o in operands), sum(o.size * o.dtype.itemsize for o in operands)
        ),
    )(*operands)


def add_body(*refs):
    count = len(refs) // 3
    for a, b, out in zip(refs[:count], refs[count : 2 * count], refs[2 * count :]):
        out[...] = (a[...].astype(F32) + b[...].astype(F32)).astype(out.dtype)


ORDERS = ((1, 0, 3, 2), (2, 3, 0, 1))


def group_body(which, *refs):
    terms, (target, *outs) = refs[:-5], refs[-5:]
    totals, sends = outs[:2], outs[2:]
    part = target.shape[0] // 2
    for c in range(2):
        value = sum(t[...].astype(F32) for t in terms[c::2])
        totals[c][...] = value
        own = target[c * part : (c + 1) * part, :].astype(F32)
        for i, b in enumerate(ORDERS[which]):
            block = value[b * part : (b + 1) * part]
            if b == 0:
                block = block - own
            sends[c][i * part : (i + 1) * part, :] = block.astype(BF)


def finish_body(*refs):
    before, got, target, rebuilt, errs = refs[:2], refs[2:4], refs[4], refs[5], refs[6:8]
    part = target.shape[0] // 2
    for c in range(2):
        rows = slice(c * part, (c + 1) * part)
        value = before[c][...] + got[c][...].astype(F32)
        rebuilt[rows, :] = value[:part].astype(BF)
        own = value[:part] - target[rows, :].astype(F32)
        errs[c][...] = jnp.concatenate([own, value[part:]], axis=0).astype(BF)


def per_device(acts, targets, enc_weight, enc_bias, dec_weight):
    layers = lax.axis_size("layer")
    layer_arr = lax.axis_index("layer").astype(jnp.int32).reshape(1)
    own_tokens, width = acts.shape[1:]
    tokens_all = own_tokens * lax.axis_size("tok")
    grad_scale = 1.0 / math.sqrt(tokens_all)
    rows = enc_weight.shape[1]
    part = own_tokens // 2
    chunks = range(2)

    def in_group(values, which):
        return [exchange(v, AXES[c][0], which) for c, v in zip(chunks, values)]

    def across(values, which):
        return [exchange(v, AXES[c][1], which) for c, v in zip(chunks, values)]

    def join(values, others):
        return [jnp.concatenate(pair, axis=0) for pair in zip(values, others)]

    group = [acts[0, c * part : (c + 1) * part] for c in chunks]
    group = join(group, in_group(group, 0))
    group = join(group, in_group(group, 1))
    *group, enc_own, dec_own, bias = tie(*group, enc_weight[0], dec_weight[0], enc_bias)
    encs = [enc_own, swap_cores(enc_own)]
    bias = jnp.concatenate([bias, swap_cores(bias)], axis=1)
    decs = [dec_own.reshape(layers * rows, width)]

    def spread(group):
        direct = across(group, 0)
        early = [*group, *direct, *across(group, 1)]
        return early, across(direct, 1)

    early, late = spread(group)
    *early, dec_own = tie(*early, decs[0])
    decs.append(swap_cores(dec_own))

    def shift(value, hop, least=0):
        if hop > 0:
            pairs = [(i, i + hop) for i in range(least, layers - hop)]
        else:
            pairs = [(i, i + hop) for i in range(max(least, -hop), layers)]
        return lax.ppermute(value, "layer", pairs)

    early_latents, early_mask, early_acts = encode(early, encs, bias)
    *late, early_latents = tie(*late, early_latents)
    latents, late_mask, late_acts = encode(late, encs, bias, [early_latents])
    one, two = shift(latents, 1), shift(latents, 2)
    hops = [latents, one, two, shift(one, 2, 1), shift(two, 2, 2)]
    hops += [shift(latents, hop) for hop in range(5, layers)]
    span, count = early_latents.shape[0], late_mask.shape[1]

    *send, late_own, late_other = recon(layer_arr, hops, span, count, decs, 2)
    late_swapped = swap_cores(late_other)
    send, late_swapped = tie(send, late_swapped)
    got = across(send, 1)
    *parts, early_own, early_other = recon(layer_arr, hops, 0, span, decs, 6)
    others = [swap_cores(early_other), late_swapped]
    target = targets[0]
    half = ((4 * part, width), BF)
    sums = ((4 * part, width), F32)
    send = vmem_call(add_body, [half] * 2, *parts[2:4], *got)
    got = across(send, 0) + across(parts[4:], 1)
    body = lambda which: functools.partial(group_body, which)
    out = vmem_call(body(1), [sums] * 2 + [half] * 2, *parts[:2], *got, target)
    out = vmem_call(body(0), [sums] * 2 + [half] * 2, *out[:2], *in_group(out[2:], 1), target)
    outs = [((own_tokens, width), BF)] + [half] * 2
    rebuilt, *errs = vmem_call(finish_body, outs, *out[:2], *in_group(out[2:], 0), target)
    early, late = spread(errs)
    *hops, early_err = latent_grads(layer_arr, decs, early, [], grad_scale, layers)
    late, hops, early_err = tie(late, hops, early_err)
    *hops, late_err = latent_grads(layer_arr, decs, late, hops, grad_scale, layers)
    relayed = [shift(hops[3], -2, 3), shift(hops[4], -2, 4)]
    lats = [early_own, others[0], late_own, others[1]]
    errs = [early_err, swap_cores(early_err), late_err, swap_cores(late_err)]
    dec_grad = dec_grads(lats, errs, grad_scale, 0)
    grads = [hops[0]] + [shift(hops[hop], -hop) for hop in range(5, layers)]
    relayed, dec_grad = tie(relayed, dec_grad)
    near = vmem_call(add_body, [(h.shape, BF) for h in hops[1:3]], *hops[1:3], *relayed)
    near, dec_grad = tie(near, dec_grad)
    grads += [shift(near[0], -1), shift(near[1], -2)]
    dec_grad = dec_grads(lats, errs, grad_scale, 1, [dec_grad])
    grads, dec_grad = tie(grads, dec_grad)
    dec_grad = dec_grad.reshape(layers, rows, width)

    mask = jnp.concatenate([early_mask, late_mask], axis=1).astype(F32)
    grad = (sum(g.astype(F32) for g in grads) * mask).astype(BF)
    early_grad, late_grad = grad[:, :span], grad[:, span:]

    def enc_part(which):
        return dot(early_grad[which], early_acts, 1, 0) + dot(late_grad[which], late_acts, 1, 0)

    got = swap_cores(enc_part(slice(rows, None)).astype(BF))
    enc_grad = (enc_part(slice(0, rows)) + got.astype(F32)).astype(BF)
    return (rebuilt[None], dec_grad[None], enc_grad[None])


def solution(mesh):
    return jax.shard_map(
        per_device,
        mesh=mesh,
        in_specs=(
            P("layer", "tok", None),
            P("layer", "tok", None),
            P("layer", "tok", None),
            P("layer", "tok"),
            P("layer", None, "tok", None),
        ),
        out_specs=(P("layer", "tok", None), P("layer", None, "tok", None), P("layer", "tok", None)),
        check_vma=False,
    )
```
